256 devices in a mesh: kvseq: 32 (over x, z), kvhead: 8 (over y, core).
Axes of the slice: x: 4, y: 4, z: 8, core: 2. Of those that a mesh axis runs over, the one named last changes fastest.
Arguments:
- residual_input: bfloat16 [8, 16384], P(None, ('kvseq', 'kvhead')), may hold values from -1210 to 1210
- norm_gain_vector: bfloat16 [16384], P(('kvseq', 'kvhead')), may hold values from 0.5 to 2
- query_weight: bfloat16 [16384, 8, 2048], P(None, 'kvhead', 'kvseq'), may hold values from -0.046875 to 0.046875
- key_value_weight: bfloat16 [16384, 8, 256], P('kvseq', 'kvhead'), may hold values from -0.046875 to 0.046875
- output_weight: bfloat16 [8, 2048, 16384], P('kvhead', None, 'kvseq'), may hold values from -0.75 to 0.75
- adapter_down_factors: bfloat16 [8, 16384, 32], P(None, 'kvhead'), may hold values from -0.046875 to 0.046875
- query_up_factors: bfloat16 [8, 16, 8, 2048], P(None, None, 'kvhead', 'kvseq'), may hold values from -1.5 to 1.5
- value_up_factors: bfloat16 [8, 16, 8, 128], P(None, None, 'kvhead'), may hold values from -1.5 to 1.5
- adapter_index: int32 [8], replicated, may hold values from 0 to 7
- lengths: int32 [8], replicated, may hold values from 4096 to 32767, as said below
- rotated_key_cache: bfloat16 [8, 32768, 8, 128], P(None, 'kvseq', 'kvhead'), may hold values from -1208 to 1208
- earlier_value_cache: bfloat16 [8, 32768, 8, 128], P(None, 'kvseq', 'kvhead'), may hold values from -24 to 24
Outputs:
- attn_delta: bfloat16 [8, 16384], P(None, ('kvseq', 'kvhead'))
- new_keyval: bfloat16 [8, 8, 256], P(None, 'kvhead')
The draws below stay inside these ranges and needn't reach their ends.
Inputs may be any that keep to these rules, and one draw needn't show every extreme that they name: Row b has lengths[b] cached positions, 0 to lengths[b] - 1, and its new token stands at position lengths[b]; some row has exactly 32767.
All inputs are finite; a program needn't handle non-finite values.
Results may differ from the reference program's by a relative error of at most 0.015.
The reference program's roundings to bfloat16 on the way count: a program that leaves them out, or rounds other values in their place, can miss the bound.
Values may be sent and summed in bfloat16 or wider, within the bound.
A program may use at most 64 MiB of HBM per device.

```python
import math
import jax
import jax.numpy as jnp
from jax import lax

MODEL_WIDTH = 16384
HEADS_PER_GROUP = 16
HEAD_SIZE = 128
ADAPTER_RANK = 16
ADAPTER_COUNT = 8
REQUEST_ROWS = 8
CTX_DEV = 1024
KEY_HEADS = 8
QUERY_HEADS = 128
CTX = 32768
N_KVSEQ = 32


def draw_residual_input(key, part):
    key = jax.random.fold_in(key, 11)
    key_base, key_cols, key_rows = jax.random.split(key, 3)
    ramp = jnp.arange(MODEL_WIDTH, dtype=jnp.float32) / MODEL_WIDTH
    base = jnp.clip(jax.random.normal(key_base, (REQUEST_ROWS, MODEL_WIDTH)), -6.0, 6.0)
    columns = jnp.exp(ramp * math.log(10.0)) * jnp.exp(jax.random.uniform(key_cols, (MODEL_WIDTH,), minval=-0.7, maxval=0.7))
    row_scale = jnp.exp(jax.random.uniform(key_rows, (REQUEST_ROWS, 1), minval=0.0, maxval=math.log(10.0)))
    return (base * columns[None, :] * row_scale).astype(jnp.bfloat16)


def draw_lengths(key, part):
    key = jax.random.fold_in(key, 23)
    key_len, key_row = jax.random.split(key, 2)
    drawn = jax.random.randint(key_len, (REQUEST_ROWS,), CTX // 8, CTX)
    longest = jax.random.randint(key_row, (), 0, REQUEST_ROWS)
    return jnp.where(jnp.arange(REQUEST_ROWS) == longest, CTX - 1, drawn).astype(jnp.int32)


def draw_rotated_key_cache(key, part):
    key = jax.random.fold_in(key, 37)
    key_base = jax.random.fold_in(key, 0)
    target_shape = (REQUEST_ROWS, CTX, KEY_HEADS, HEAD_SIZE)
    result = jnp.clip(jax.random.normal(key_base, target_shape), -6.0, 6.0)
    return result.astype(jnp.bfloat16)


def with_ends(values, own_key, low, top_value):
    shape = values.shape
    index_at = [jax.random.randint(jax.random.fold_in(own_key, axis), (), 0, shape[axis]) for axis in range(len(shape))]
    values = values.at[tuple(index_at)].set(low)
    longest = shape.index(max(shape))
    index_at[longest] = (index_at[longest] + 1) % shape[longest]
    return values.at[tuple(index_at)].set(top_value)


def spiked(values, rng, source, target, blocks, factor):
    owner, partner = [(jnp.arange(values.shape[dim]) // (values.shape[dim] // blocks)).reshape([-1 if axis == dim else 1 for axis in range(values.ndim)]) for dim in (source, target)]
    chosen = jax.random.permutation(rng, blocks)[partner]
    strong = (owner == chosen) | (owner == (partner + blocks // 2) % blocks)
    return jnp.where(strong, factor * values, values)


def level_of(key, extent, shards, least, top_value):
    factor_of, own = 1.0, jax.random.fold_in(key, 6)
    for dim, blocks in shards:
        draws = jnp.exp(jax.random.uniform(jax.random.fold_in(own, dim), (blocks,), jnp.float32, least / len(shards), top_value / len(shards)))
        factor_of = factor_of * jnp.repeat(draws, extent[dim] // blocks).reshape([-1 if axis == dim else 1 for axis in range(len(extent))])
    return factor_of


def scatter_about(own_key, dims, width, limit, pieces=(), held_as=jnp.bfloat16):
    values = width * jax.random.normal(own_key, dims, jnp.float32)
    if pieces:
        values = values * level_of(own_key, dims, pieces, -0.22, 0.18)
    return jnp.clip(values, -limit, limit).astype(held_as)


def heavy_noise(key, dims, deviation, limit, pieces, heavy, kind=jnp.bfloat16):
    entries = deviation * jax.random.normal(key, dims, jnp.float32)
    if pieces:
        entries = entries * level_of(key, dims, pieces, -0.22, 0.18)
    return jnp.clip(spiked(entries, jax.random.fold_in(key, 3), *heavy), -limit, limit).astype(kind)


def setup_inputs(seed: int = 0) -> dict:
    keys = jax.random.split(jax.random.key(seed), 13)
    residual_input = draw_residual_input(jax.random.fold_in(keys[12], 71), 0)
    norm_gain_vector = jnp.clip(jnp.exp(math.log(2.0) - 1.3862944 * jax.random.uniform(keys[1], (MODEL_WIDTH,), jnp.float32) ** level_of(keys[1], (MODEL_WIDTH,), ((0, 256),), -0.2, 0.2)), 0.5, 2.0).astype(jnp.bfloat16)
    query_weight = scatter_about(keys[2], (MODEL_WIDTH, KEY_HEADS, HEADS_PER_GROUP * HEAD_SIZE), MODEL_WIDTH ** -0.5, 0.046875, ((1, 8), (2, 32)))
    key_value_weight = scatter_about(keys[3], (MODEL_WIDTH, KEY_HEADS, 2 * HEAD_SIZE), MODEL_WIDTH ** -0.5, 0.046875, ((0, 32), (1, 8)))
    output_weight = heavy_noise(keys[4], (KEY_HEADS, HEADS_PER_GROUP * HEAD_SIZE, MODEL_WIDTH), HEAD_SIZE ** -0.5, 0.75, ((0, 8), (2, 32)), (0, 2, 8, 2.0))
    adapter_down_factors = scatter_about(keys[5], (ADAPTER_COUNT, MODEL_WIDTH, 2 * ADAPTER_RANK), MODEL_WIDTH ** -0.5, 0.046875, ((1, 8),))
    query_up_factors = scatter_about(keys[6], (ADAPTER_COUNT, ADAPTER_RANK, KEY_HEADS, HEADS_PER_GROUP * HEAD_SIZE), ADAPTER_RANK ** -0.5, 1.5, ((2, 8), (3, 32)))
    value_up_factors = scatter_about(keys[7], (ADAPTER_COUNT, ADAPTER_RANK, KEY_HEADS, HEAD_SIZE), ADAPTER_RANK ** -0.5, 1.5, ((2, 8),))
    adapter_index = with_ends(jax.random.randint(keys[8], (REQUEST_ROWS,), 0, ADAPTER_COUNT), jax.random.fold_in(keys[8], 1), 0, ADAPTER_COUNT - 1).astype(jnp.int32)
    lengths = draw_lengths(jax.random.fold_in(keys[12], 71), 0)
    rotated_key_cache = draw_rotated_key_cache(jax.random.fold_in(keys[12], 71), 0)
    earlier_value_cache = scatter_about(keys[11], (REQUEST_ROWS, CTX, KEY_HEADS, HEAD_SIZE), 4.0, 24.0, ((1, 32), (2, 8)))
    return dict(residual_input=residual_input, norm_gain_vector=norm_gain_vector, query_weight=query_weight, key_value_weight=key_value_weight, output_weight=output_weight, adapter_down_factors=adapter_down_factors, query_up_factors=query_up_factors, value_up_factors=value_up_factors, adapter_index=adapter_index, lengths=lengths, rotated_key_cache=rotated_key_cache, earlier_value_cache=earlier_value_cache)


epsilon = 1e-05
rope_base = 500000.0
masked_fill = -1e+30

def rotary(vector, position):
    half_dim = vector.shape[-1] // 2
    frequency = jnp.exp(jnp.arange(half_dim, dtype=jnp.float32) * (-math.log(rope_base) / half_dim))
    angles = position * frequency
    cosine = jnp.cos(angles)
    sine_part = jnp.sin(angles)
    former = vector[..., :half_dim]
    latter = vector[..., half_dim:]
    return jnp.concatenate([former * cosine - latter * sine_part, latter * cosine + former * sine_part], axis=-1)

def reference(residual_input, norm_gain_vector, query_weight, key_value_weight, output_weight, adapter_down_factors, query_up_factors, value_up_factors, adapter_index, lengths, rotated_key_cache, earlier_value_cache):
    widened = residual_input.astype(jnp.float32)
    mean_square = lax.optimization_barrier(jnp.sum(widened * widened, axis=1, keepdims=True)) / MODEL_WIDTH
    normed = (widened * lax.rsqrt(mean_square + epsilon) * norm_gain_vector.astype(jnp.float32)[None, :]).astype(jnp.bfloat16)
    adapter_library = adapter_down_factors[adapter_index]
    low_rank = jnp.einsum('bd,bdr->br', normed.astype(jnp.float32), adapter_library.astype(jnp.float32), precision=lax.Precision.HIGHEST).astype(jnp.bfloat16)
    query_reduced = low_rank[:, :ADAPTER_RANK].astype(jnp.float32)
    value_reduced = low_rank[:, ADAPTER_RANK:].astype(jnp.float32)
    query_plain = jnp.dot(normed, query_weight.reshape(MODEL_WIDTH, QUERY_HEADS * HEAD_SIZE), preferred_element_type=jnp.float32)
    query_adapter_delta = jnp.einsum('us,use->ue', query_reduced, query_up_factors[adapter_index].reshape(REQUEST_ROWS, ADAPTER_RANK, QUERY_HEADS * HEAD_SIZE).astype(jnp.float32), precision=lax.Precision.HIGHEST)
    query_matrix = (query_plain + query_adapter_delta).astype(jnp.bfloat16)
    key_value_rows = jnp.dot(normed, key_value_weight.reshape(MODEL_WIDTH, KEY_HEADS * 2 * HEAD_SIZE), preferred_element_type=jnp.float32).reshape(REQUEST_ROWS, KEY_HEADS, 2 * HEAD_SIZE)
    value_adapter_delta = jnp.einsum('oy,oypt->opt', value_reduced, value_up_factors[adapter_index].astype(jnp.float32), precision=lax.Precision.HIGHEST)
    fresh_value = key_value_rows[:, :, HEAD_SIZE:] + value_adapter_delta
    position = lengths.astype(jnp.float32)
    key_new = rotary(key_value_rows[:, :, :HEAD_SIZE], position[:, None, None])
    new_keyval = jnp.concatenate([key_new, fresh_value], axis=-1).astype(jnp.bfloat16)
    q_rot = rotary(query_matrix.astype(jnp.float32).reshape(REQUEST_ROWS, KEY_HEADS, HEADS_PER_GROUP, HEAD_SIZE), position[:, None, None, None]).astype(jnp.bfloat16)
    score_scale = 1.0 / math.sqrt(HEAD_SIZE)
    positions = jnp.arange(CTX, dtype=jnp.int32).reshape(N_KVSEQ, CTX_DEV)

    def attend_group(kv_group):
        queries = lax.dynamic_index_in_dim(q_rot, kv_group, 1, keepdims=False).astype(jnp.float32)
        key_rows = lax.dynamic_index_in_dim(rotated_key_cache, kv_group, 2, keepdims=False).astype(jnp.float32).reshape(REQUEST_ROWS, N_KVSEQ, CTX_DEV, HEAD_SIZE)
        value_rows = lax.dynamic_index_in_dim(earlier_value_cache, kv_group, 2, keepdims=False).astype(jnp.float32).reshape(REQUEST_ROWS, N_KVSEQ, CTX_DEV, HEAD_SIZE)
        own_row = lax.dynamic_index_in_dim(new_keyval, kv_group, 1, keepdims=False).astype(jnp.float32)
        scores = jnp.einsum('bqh,bnph->bqnp', queries, key_rows) * score_scale
        is_valid = positions[None, None, :, :] < lengths[:, None, None, None]
        masked = jnp.where(is_valid, scores, masked_fill)
        block_max = lax.optimization_barrier(jnp.max(masked, axis=3))
        weights = jnp.where(is_valid, jnp.exp(masked - block_max[..., None]), 0.0)
        block_total = lax.optimization_barrier(jnp.sum(weights, axis=3))
        block_acc = jnp.einsum('bqnp,bnph->bqnh', weights.astype(jnp.bfloat16).astype(jnp.float32), value_rows)
        self_score = jnp.einsum('bqh,bh->bq', queries, own_row[:, :HEAD_SIZE]) * score_scale
        highest = jnp.maximum(lax.optimization_barrier(jnp.max(block_max, axis=2)), self_score)
        factor = jnp.exp(block_max - highest[..., None])
        self_weight = jnp.exp(self_score - highest)
        summed = lax.optimization_barrier(jnp.sum(factor * block_total, axis=2)) + self_weight
        weighted = lax.optimization_barrier(jnp.sum(factor[..., None] * block_acc, axis=2)) + self_weight[..., None] * own_row[:, None, HEAD_SIZE:]
        return weighted / summed[..., None]
    attended = lax.map(attend_group, jnp.arange(KEY_HEADS, dtype=jnp.int32))
    attended = jnp.transpose(attended, (1, 0, 2, 3)).reshape(REQUEST_ROWS, QUERY_HEADS * HEAD_SIZE).astype(jnp.bfloat16)
    attn_delta = jnp.dot(attended, output_weight.reshape(QUERY_HEADS * HEAD_SIZE, MODEL_WIDTH), preferred_element_type=jnp.float32).astype(jnp.bfloat16)
    return (attn_delta, new_keyval)
```

```python
import math

import jax
import jax.numpy as jnp
import numpy as np
from jax import lax
from jax.experimental import pallas as pl
from jax.experimental.pallas import tpu as pltpu
from jax.sharding import PartitionSpec as P

MODEL_WIDTH = 16384
HEADS = 16
HEAD_SIZE = 128
HALF = HEAD_SIZE // 2
ADAPTERS = 8
RANK = 16
ROWS = 8
SPAN = 1024
NX, NY, NZ, NC = 4, 4, 8, 2
SEQ = NX * NZ
GROUPS = NY * NC
QUADS = SEQ // ROWS

EPSILON = 1e-05
ROPE_BASE = 500000.0
MASKED = -1e30
SCORE_SCALE = 1.0 / math.sqrt(HEAD_SIZE)
MESH = pl.DeviceIdType.MESH
F32 = jnp.float32
BF16 = jnp.bfloat16
NT = (((1,), (1,)), ((), ()))


def ring(k, n):
    return min(k, n - k)


def offsets(xs, ys, zs, cs):
    found = [(x, y, z, c) for x in xs for y in ys for z in zs for c in cs if (x, y, z, c) != (0, 0, 0, 0)]
    return sorted(found, key=lambda o: (-(ring(o[0], NX) + ring(o[1], NY) + ring(o[2], NZ)), -o[3]))


Z_PARTNERS = offsets([0], [0], range(NZ), range(NC))
XY_PARTNERS = offsets(range(NX), range(NY), [0], [0])
HEAD_PARTNERS = offsets([0], range(NY), [0], range(NC))
SEQ_PARTNERS = offsets(range(NX), [0], range(NZ), [0])


def kernel(
    x_hbm, gain_hbm, qw_hbm, kvw_hbm, ow_hbm, down_hbm, qup_hbm, vup_hbm, adapter_hbm, length_hbm, k_hbm, v_hbm, freq_hbm,
    out_ref, kv_ref,
    x_v, gain_v, qw_v, kvw_v, ow_v, down_v, qup_v, vup_v, adapter_s, length_s, k_v, v_v, freq_v,
    z_msg, z_buf, xy_buf, normed, b_buf, c_msg, c_buf, q_rot, d_msg, d_buf, kv_rows, e_buf, f_msg, f_buf,
    local_sem, send_sem, recv_sem,
):
    seq, head = lax.axis_index("kvseq"), lax.axis_index("kvhead")
    x, z = seq // NZ, lax.rem(seq, NZ)
    y, c = head // NC, lax.rem(head, NC)

    def place(o):
        px, pz = lax.rem(x + o[0], NX), lax.rem(z + o[2], NZ)
        py, pc = lax.rem(y + o[1], NY), lax.rem(c + o[3], NC)
        return px * NZ + pz, py * NC + pc

    barrier = pltpu.get_barrier_semaphore()
    for o in XY_PARTNERS + Z_PARTNERS:
        pl.semaphore_signal(barrier, inc=1, device_id=place(o), device_id_type=MESH)

    fetches = {}
    for n, (name, src, dst) in enumerate([
        ("x", x_hbm, x_v), ("gain", gain_hbm, gain_v), ("adapter", adapter_hbm, adapter_s), ("length", length_hbm, length_s),
        ("freq", freq_hbm, freq_v), ("down", down_hbm, down_v), ("qw", qw_hbm, qw_v), ("kvw", kvw_hbm, kvw_v),
        ("qup", qup_hbm, qup_v.at[:, pl.ds(0, RANK)]), ("vup", vup_hbm, vup_v.at[:, pl.ds(RANK, RANK)]),
        ("k", k_hbm, k_v), ("v", v_hbm, v_v), ("ow", ow_hbm, ow_v),
    ]):
        fetches[name] = pltpu.make_async_copy(src, dst, local_sem.at[n])
        fetches[name].start()

    sent = []

    def send(phase, o, src, dst):
        copy = pltpu.make_async_remote_copy(
            src_ref=src, dst_ref=dst, send_sem=send_sem.at[phase], recv_sem=recv_sem.at[phase],
            device_id=place(o), device_id_type=MESH,
        )
        copy.start()

    def landed(phase, ref, sem=None):
        pltpu.make_async_copy(ref, ref, recv_sem.at[phase]).wait()
        sent.append((phase, ref))

    lane = lax.broadcasted_iota(jnp.int32, (ROWS, 128), 1)
    sub = lax.broadcasted_iota(jnp.int32, (ROWS, 128), 0)

    fetches["x"].wait()
    fetches["gain"].wait()
    mine = x_v[...].astype(F32)
    gains = jnp.broadcast_to(gain_v[...].astype(F32).reshape(1, HALF), (ROWS, HALF))
    both = jnp.concatenate([mine, jnp.where(sub[:, :HALF] == 0, gains, 0.0)], axis=0)
    both = jnp.concatenate([both, both], axis=1)
    lane2 = lax.broadcasted_iota(jnp.int32, (2 * ROWS, 128), 1)
    block = jnp.where(lane2 // HALF == c, both, 0.0).astype(BF16)
    z_msg[...] = block
    z_buf[pl.ds(z * NC + c, 1)] = block[None]

    pl.semaphore_wait(barrier, len(XY_PARTNERS) + len(Z_PARTNERS))
    for o in Z_PARTNERS:
        send(0, o, z_msg, z_buf.at[z * NC + c])

    fetches["length"].wait()
    fetches["freq"].wait()
    fetches["adapter"].wait()
    position = jnp.zeros((ROWS, 128), F32)
    adapter = jnp.zeros((ROWS, ADAPTERS * 2 * RANK), jnp.int32)
    sub_wide = lax.broadcasted_iota(jnp.int32, adapter.shape, 0)
    for b in range(ROWS):
        position = jnp.where(sub == b, length_s[b].astype(F32), position)
        adapter = jnp.where(sub_wide == b, adapter_s[b], adapter)
    chosen = adapter == lax.broadcasted_iota(jnp.int32, adapter.shape, 1) // (2 * RANK)
    angles = position * freq_v[...]
    cosine, sine = jnp.cos(angles), jnp.sin(angles)
    qup_v[:, RANK:, :] = jnp.zeros((ADAPTERS, RANK, HALF), BF16)
    vup_v[:, :RANK, :] = jnp.zeros((ADAPTERS, RANK, HEAD_SIZE), BF16)

    landed(0, z_buf.at[pl.ds(0, NZ * NC - 1)])
    tiles = [z_buf[2 * k].astype(F32) + z_buf[2 * k + 1].astype(F32) for k in range(NZ)]
    packed = [jnp.concatenate([tiles[k][:ROWS], tiles[k + 1][:ROWS]], axis=0) for k in range(0, NZ, 2)]
    gain_rows = jnp.zeros((2 * ROWS, 128), F32)
    sub2 = lax.broadcasted_iota(jnp.int32, gain_rows.shape, 0)
    for k in range(NZ):
        gain_rows = jnp.where(sub2 == k, tiles[k][ROWS : ROWS + 1], gain_rows)
    xy_mine = xy_buf.at[x * NY + y]
    xy_mine[...] = jnp.concatenate(packed + [gain_rows], axis=0).astype(BF16)
    for o in XY_PARTNERS:
        send(1, o, xy_mine, xy_mine)
    landed(1, xy_buf.at[pl.ds(0, NX * NY - 1)])

    squares = jnp.zeros((2 * ROWS, 128), F32)
    for k in range(NX * NY):
        for p in range(NZ // 2):
            part = xy_buf[k, pl.ds(2 * ROWS * p, 2 * ROWS)].astype(F32)
            squares = squares + part * part
    square_sum = jnp.sum(squares[:ROWS] + squares[ROWS:], axis=1, keepdims=True)
    scaling = jnp.broadcast_to(lax.rsqrt(square_sum / MODEL_WIDTH + EPSILON), (ROWS, 128))
    scaling = jnp.concatenate([scaling, scaling], axis=0)
    for k in range(NX * NY):
        kx, ky = k // NY, k % NY
        gain_k = xy_buf[k, pl.ds(NZ * ROWS, 2 * ROWS)].astype(F32)
        for p in range(NZ // 2):
            part = xy_buf[k, pl.ds(2 * ROWS * p, 2 * ROWS)].astype(F32) * scaling
            for i in range(2):
                kz = 2 * p + i
                tile = (kx * NZ + kz) * NY + ky
                normed[:, pl.ds(tile * 128, 128)] = (part[i * ROWS : (i + 1) * ROWS] * gain_k[kz : kz + 1]).astype(BF16)

    fetches["down"].wait()
    low_width = MODEL_WIDTH // GROUPS
    low_part = lax.dot_general(
        normed[:, pl.ds(pl.multiple_of(head * low_width, low_width), low_width)],
        down_v[...].reshape(ADAPTERS * 2 * RANK, low_width), NT, preferred_element_type=F32,
    )
    b_mine = b_buf.at[head]
    b_mine[...] = low_part
    for o in HEAD_PARTNERS:
        send(2, o, b_mine, b_mine)

    fetches["kvw"].wait()
    seq_width = MODEL_WIDTH // SEQ
    keyval_part = jnp.dot(
        normed[:, pl.ds(pl.multiple_of(seq * seq_width, seq_width), seq_width)], kvw_v[...], preferred_element_type=F32
    )
    fetches["qw"].wait()
    query_plain = lax.dot_general(normed[...], qw_v[...], NT, preferred_element_type=F32)
    fetches["qup"].wait()
    fetches["vup"].wait()

    landed(2, b_buf.at[pl.ds(0, GROUPS - 1)])
    low_sum = b_buf[0]
    for k in range(1, GROUPS):
        low_sum = low_sum + b_buf[k]
    low_rank = jnp.where(chosen, low_sum, 0.0).astype(BF16)
    query_delta = jnp.dot(
        low_rank, qup_v[...].reshape(ADAPTERS * 2 * RANK, HALF), preferred_element_type=F32
    )
    query_mine = (query_plain + query_delta).astype(BF16).astype(F32)
    for k in range(4):
        c_msg[k] = jnp.concatenate([query_mine, keyval_part[:, k * HALF : (k + 1) * HALF]], axis=1)
    c_buf[pl.ds(seq, 1)] = c_msg[pl.ds(lax.rem(z, 4), 1)]
    for o in SEQ_PARTNERS:
        send(3, o, c_msg.at[lax.rem(z + o[2], 4)], c_buf.at[seq])
    value_delta = jnp.dot(
        low_rank, vup_v[...].reshape(ADAPTERS * 2 * RANK, HEAD_SIZE), preferred_element_type=F32
    )

    landed(3, c_buf.at[pl.ds(0, SEQ - 1)])
    kv_sum = c_buf[0]
    for k in range(1, SEQ):
        kv_sum = kv_sum + c_buf[k]
    kv_rows[...] = kv_sum
    kv_piece = jnp.broadcast_to(kv_rows[pl.ds(seq // QUADS, 1)], (HEADS, 128))
    for h in range(HEADS):
        former, latter = c_buf[2 * h], c_buf[2 * h + 1]
        first = former * cosine - latter * sine
        second = latter * cosine + former * sine
        turned = jnp.concatenate([first[:, :HALF], second[:, :HALF]], axis=1)
        q_rot[pl.ds(h * ROWS, ROWS)] = turned.astype(BF16).astype(F32)

    fetches["k"].wait()
    fetches["v"].wait()
    where = seq * SPAN + lax.broadcasted_iota(jnp.int32, (HEADS, SPAN), 1)
    lane_h = lax.broadcasted_iota(jnp.int32, (HEADS, 128), 1)
    for b in range(ROWS):
        queries = q_rot[pl.ds(b, HEADS, stride=ROWS)].astype(BF16)
        scores = lax.dot_general(queries, k_v[b], NT, preferred_element_type=F32) * SCORE_SCALE
        valid = where < length_s[b]
        masked = jnp.where(valid, scores, MASKED)
        block_max = jnp.max(masked, axis=1, keepdims=True)
        weights = jnp.where(valid, jnp.exp(masked - block_max), 0.0)
        block_total = jnp.sum(weights, axis=1, keepdims=True)
        block_acc = jnp.dot(weights.astype(BF16), v_v[b], preferred_element_type=F32)
        facts = jnp.where(lane_h < 32, block_max, jnp.where(lane_h < 64, block_total, kv_piece))
        for k in range(QUADS):
            d_msg[b * QUADS + k, pl.ds(0, 4)] = block_acc[4 * k : 4 * k + 4]
            d_msg[b * QUADS + k, pl.ds(4, 4)] = facts[4 * k : 4 * k + 4]
    own = pl.ds(pl.multiple_of(seq * 8, 8), 8)
    d_buf[own] = d_msg[pl.ds(seq, 1)].reshape(8, 128)
    for o in SEQ_PARTNERS:
        send(4, o, d_msg.at[place(o)[0]], d_buf.at[own])
    landed(4, d_buf.at[pl.ds(0, (SEQ - 1) * 8)])

    quarter = [d_buf[pl.ds(8 * k + 4, ROWS, stride=8 * QUADS)] for k in range(4)]
    key_first = quarter[0] * cosine - quarter[1] * sine
    key_second = quarter[1] * cosine + quarter[0] * sine
    key_new = jnp.concatenate([key_first[:, HALF:], key_second[:, HALF:]], axis=1).astype(BF16)
    value_new = (jnp.concatenate([quarter[2][:, HALF:], quarter[3][:, HALF:]], axis=1) + value_delta).astype(BF16)
    kv_ref[:, pl.ds(0, HEAD_SIZE)] = key_new
    kv_ref[:, pl.ds(HEAD_SIZE, HEAD_SIZE)] = value_new

    row, quad = seq // QUADS, lax.rem(seq, QUADS)
    kv_rows[...] = key_new.astype(F32)
    own_key = kv_rows[pl.ds(row, 1)]
    kv_rows[...] = value_new.astype(F32)
    own_value = kv_rows[pl.ds(row, 1)]
    own_queries = q_rot[pl.ds(quad * 4 * ROWS + row, 4, stride=ROWS)]
    self_score = jnp.sum(own_queries * own_key, axis=1, keepdims=True) * SCORE_SCALE
    e_rows = []
    for j in range(4):
        acc = d_buf[pl.ds(j, SEQ, stride=8)]
        facts = d_buf[pl.ds(4 + j, SEQ, stride=8)]
        peaks = jnp.broadcast_to(facts[:, :1], (SEQ, 128))
        own_score = jnp.broadcast_to(self_score[j : j + 1], (1, 128))
        highest = jnp.maximum(jnp.max(peaks, axis=0, keepdims=True), own_score)
        factor = jnp.exp(peaks - highest)
        self_weight = jnp.exp(own_score - highest)
        summed = jnp.sum(factor * facts, axis=0, keepdims=True)
        summed = jnp.broadcast_to(summed[:, 32:33], (1, 128)) + self_weight
        weighted = jnp.sum(factor * acc, axis=0, keepdims=True) + self_weight * own_value
        e_rows.append(weighted / summed)
    attended_own = jnp.concatenate(e_rows + e_rows, axis=0).astype(BF16).astype(F32)
    e_buf[own] = attended_own
    for o in SEQ_PARTNERS:
        send(5, o, e_buf.at[own], e_buf.at[own])
    fetches["ow"].wait()
    landed(5, e_buf.at[pl.ds(0, (SEQ - 1) * 8)])

    attended = jnp.concatenate(
        [e_buf[pl.ds(8 * (h // 4) + h % 4, ROWS, stride=8 * QUADS)] for h in range(HEADS)], axis=1
    ).astype(BF16)
    partial = jnp.dot(attended, ow_v[...], preferred_element_type=F32)
    for k in range(GROUPS):
        tile = partial[:, 128 * (k // 2) : 128 * (k // 2) + 128]
        if k % 2:
            tile = pltpu.roll(tile, HALF, 1)
        f_msg[k] = tile
    f_buf[pl.ds(head, 1)] = f_msg[pl.ds(head, 1)]
    for o in HEAD_PARTNERS:
        send(6, o, f_msg.at[place(o)[1]], f_buf.at[head])
    landed(6, f_buf.at[pl.ds(0, GROUPS - 1)])
    total = f_buf[0]
    for k in range(1, GROUPS):
        total = total + f_buf[k]
    out_ref[...] = total[:, :HALF].astype(BF16)
    for phase, ref in sent:
        pltpu.make_async_copy(ref, ref, send_sem.at[phase]).wait()


def local(
    residual_input,
    norm_gain_vector,
    query_weight,
    key_value_weight,
    output_weight,
    adapter_down_factors,
    query_up_factors,
    value_up_factors,
    adapter_index,
    lengths,
    rotated_key_cache,
    earlier_value_cache,
):
    frequency = np.exp(np.arange(HALF, dtype=np.float64) * (-math.log(ROPE_BASE) / HALF)).astype(np.float32)
    frequency = jnp.asarray(np.concatenate([frequency, frequency])[None, :])
    operands = (
        residual_input,
        norm_gain_vector,
        jnp.transpose(query_weight, (1, 2, 0)).reshape(HALF, MODEL_WIDTH),
        key_value_weight.reshape(MODEL_WIDTH // SEQ, 2 * HEAD_SIZE),
        output_weight.reshape(HEADS * HEAD_SIZE, MODEL_WIDTH // SEQ),
        jnp.transpose(adapter_down_factors, (0, 2, 1)),
        query_up_factors.reshape(ADAPTERS, RANK, HALF),
        value_up_factors.reshape(ADAPTERS, RANK, HEAD_SIZE),
        adapter_index,
        lengths,
        rotated_key_cache.reshape(ROWS, SPAN, HEAD_SIZE),
        earlier_value_cache.reshape(ROWS, SPAN, HEAD_SIZE),
        frequency,
    )
    dma, vmem = pltpu.SemaphoreType.DMA, pltpu.VMEM
    attn_delta, new_keyval = pl.pallas_call(
        kernel,
        out_shape=(
            jax.ShapeDtypeStruct((ROWS, HALF), BF16),
            jax.ShapeDtypeStruct((ROWS, 2 * HEAD_SIZE), BF16),
        ),
        in_specs=[pl.BlockSpec(memory_space=pl.ANY)] * len(operands),
        out_specs=(pl.BlockSpec(memory_space=vmem), pl.BlockSpec(memory_space=vmem)),
        scratch_shapes=[
            vmem((ROWS, HALF), BF16),
            vmem((HALF,), BF16),
            vmem((HALF, MODEL_WIDTH), BF16),
            vmem((MODEL_WIDTH // SEQ, 2 * HEAD_SIZE), BF16),
            vmem((HEADS * HEAD_SIZE, MODEL_WIDTH // SEQ), BF16),
            vmem((ADAPTERS, 2 * RANK, MODEL_WIDTH // GROUPS), BF16),
            vmem((ADAPTERS, 2 * RANK, HALF), BF16),
            vmem((ADAPTERS, 2 * RANK, HEAD_SIZE), BF16),
            pltpu.SMEM((ADAPTERS,), jnp.int32),
            pltpu.SMEM((ROWS,), jnp.int32),
            vmem((ROWS, SPAN, HEAD_SIZE), BF16),
            vmem((ROWS, SPAN, HEAD_SIZE), BF16),
            vmem((1, 128), F32),
            vmem((2 * ROWS, 128), BF16),
            vmem((NZ * NC, 2 * ROWS, 128), BF16),
            vmem((NX * NY, NZ * ROWS + 2 * ROWS, 128), BF16),
            vmem((ROWS, MODEL_WIDTH), BF16),
            vmem((GROUPS, ROWS, ADAPTERS * 2 * RANK), F32),
            vmem((4, ROWS, 128), F32),
            vmem((SEQ, ROWS, 128), F32),
            vmem((HEADS * ROWS, 128), F32),
            vmem((SEQ, 8, 128), F32),
            vmem((SEQ * 8, 128), F32),
            vmem((ROWS, 128), F32),
            vmem((SEQ * 8, 128), F32),
            vmem((GROUPS, ROWS, 128), F32),
            vmem((GROUPS, ROWS, 128), F32),
            dma((13,)),
            dma((7,)),
            dma((7,)),
        ],
        compiler_params=pltpu.CompilerParams(
            collective_id=0, has_side_effects=True, vmem_limit_bytes=62 * 2**20
        ),
        name="decode_attention",
    )(*operands)
    return attn_delta, new_keyval[:, None, :]


def solution(mesh):
    return jax.shard_map(
        local,
        mesh=mesh,
        in_specs=(
            P(None, ("kvseq", "kvhead")),
            P(("kvseq", "kvhead")),
            P(None, "kvhead", "kvseq"),
            P("kvseq", "kvhead", None),
            P("kvhead", None, "kvseq"),
            P(None, "kvhead", None),
            P(None, None, "kvhead", "kvseq"),
            P(None, None, "kvhead", None),
            P(),
            P(),
            P(None, "kvseq", "kvhead", None),
            P(None, "kvseq", "kvhead", None),
        ),
        out_specs=(P(None, ("kvseq", "kvhead")), P(None, "kvhead", None)),
        check_vma=False,
    )
```

```python
import math

import jax
import jax.numpy as jnp
import numpy as np
from jax import lax
from jax.experimental import pallas as pl
from jax.experimental.pallas import tpu as pltpu
from jax.sharding import PartitionSpec as P

MODEL_WIDTH = 16384
HEADS = 16
HEAD_SIZE = 128
HALF = HEAD_SIZE // 2
ADAPTERS = 8
RANK = 16
ROWS = 8
SPAN = 1024
NX, NY, NZ, NC = 4, 4, 8, 2
SEQ = NX * NZ
GROUPS = NY * NC
QUADS = SEQ // ROWS

EPSILON = 1e-05
ROPE_BASE = 500000.0
MASKED = -1e30
SCORE_SCALE = 1.0 / math.sqrt(HEAD_SIZE)
MESH = pl.DeviceIdType.MESH
F32 = jnp.float32
BF16 = jnp.bfloat16
NT = (((1,), (1,)), ((), ()))


def ring(k, n):
    return min(k, n - k)


def added(terms):
    while len(terms) > 1:
        terms = [sum(terms[k + 1 : k + 2], terms[k]) for k in range(0, len(terms), 2)]
    return terms[0]


def offsets(xs, ys, zs, cs):
    found = [(x, y, z, c) for x in xs for y in ys for z in zs for c in cs if (x, y, z, c) != (0, 0, 0, 0)]
    return sorted(found, key=lambda o: (-(ring(o[0], NX) + ring(o[1], NY) + ring(o[2], NZ)), -o[3]))


Z_PARTNERS = offsets([0], [0], range(NZ), range(NC))
XY_PARTNERS = offsets(range(NX), range(NY), [0], [0])
HEAD_PARTNERS = offsets([0], range(NY), [0], range(NC))
SEQ_PARTNERS = offsets(range(NX), [0], range(NZ), [0])


def kernel(
    x_hbm, gain_hbm, qw_hbm, kvw_hbm, ow_hbm, down_hbm, qup_hbm, vup_hbm, adapter_hbm, length_hbm, k_hbm, v_hbm, freq_hbm,
    out_ref, kv_ref,
    x_v, gain_v, qw_v, kvw_v, ow_v, down_v, qup_v, vup_v, adapter_s, length_s, k_v, v_v, freq_v,
    z_msg, z_buf, xy_buf, sq_buf, group_in, normed, b_buf, c_msg, c_buf, q_rot, d_msg, d_buf, kv_rows, e_buf, f_msg, f_buf,
    local_sem, send_sem, recv_sem, xy_sem,
):
    seq, head = lax.axis_index("kvseq"), lax.axis_index("kvhead")
    x, z = seq // NZ, lax.rem(seq, NZ)
    y, c = head // NC, lax.rem(head, NC)

    at_x = [lax.rem(x + k, NX) for k in range(NX)]
    at_y = [lax.rem(y + k, NY) for k in range(NY)]
    at_z = [lax.rem(z + k, NZ) for k in range(NZ)]
    at_c = [c, 1 - c]
    at_seq = [[at_x[i] * NZ + at_z[k] for k in range(NZ)] for i in range(NX)]
    at_head = [[at_y[i] * NC + at_c[k] for k in range(NC)] for i in range(NY)]

    def place(o):
        return at_seq[o[0]][o[2]], at_head[o[1]][o[3]]

    barrier = pltpu.get_barrier_semaphore()
    for o in XY_PARTNERS + Z_PARTNERS:
        pl.semaphore_signal(barrier, inc=1, device_id=place(o), device_id_type=MESH)

    fetches = {}

    def fetch(name, src, dst):
        fetches[name] = pltpu.make_async_copy(src, dst, local_sem.at[len(fetches)])
        fetches[name].start()

    fetch("x", x_hbm, x_v)
    fetch("gain", gain_hbm, gain_v)
    fetch("length", length_hbm, length_s)
    fetch("adapter", adapter_hbm, adapter_s)
    fetch("freq", freq_hbm, freq_v)

    sent = []

    def send_to(phase, device, src, dst, sem):
        copy = pltpu.make_async_remote_copy(
            src_ref=src, dst_ref=dst, send_sem=send_sem.at[phase], recv_sem=sem, device_id=device, device_id_type=MESH
        )
        copy.start()

    def send(phase, o, src, dst):
        send_to(phase, place(o), src, dst, recv_sem.at[phase])

    def landed(phase, ref):
        pltpu.make_async_copy(ref, ref, recv_sem.at[phase]).wait()
        sent.append((phase, ref))

    lane = lax.broadcasted_iota(jnp.int32, (ROWS, 128), 1)
    sub = lax.broadcasted_iota(jnp.int32, (ROWS, 128), 0)

    fetches["x"].wait()
    fetches["gain"].wait()
    mine = x_v[...].astype(F32)
    gains = jnp.broadcast_to(gain_v[...].astype(F32).reshape(1, HALF), (ROWS, HALF))
    both = jnp.concatenate([mine, jnp.where(sub[:, :HALF] == 0, gains, 0.0)], axis=0)
    both = jnp.concatenate([both, both], axis=1)
    lane2 = lax.broadcasted_iota(jnp.int32, (2 * ROWS, 128), 1)
    block = jnp.where(lane2 // HALF == c, both, 0.0).astype(BF16)
    z_msg[...] = block
    z_buf[pl.ds(z * NC + c, 1)] = block[None]

    pl.semaphore_wait(barrier, len(XY_PARTNERS) + len(Z_PARTNERS))
    for o in Z_PARTNERS:
        send(0, o, z_msg, z_buf.at[z * NC + c])
    fetch("down", down_hbm, down_v)
    fetch("kvw", kvw_hbm, kvw_v)
    fetch("qw", qw_hbm, qw_v)
    fetch("qup", qup_hbm, qup_v.at[:, pl.ds(0, RANK)])
    fetch("vup", vup_hbm, vup_v.at[:, pl.ds(RANK, RANK)])
    fetch("k", k_hbm, k_v)
    fetch("v", v_hbm, v_v)
    fetch("ow", ow_hbm, ow_v)

    fetches["length"].wait()
    fetches["freq"].wait()
    fetches["adapter"].wait()
    position = jnp.zeros((ROWS, 128), F32)
    adapter = jnp.zeros((ROWS, ADAPTERS * 2 * RANK), jnp.int32)
    sub_wide = lax.broadcasted_iota(jnp.int32, adapter.shape, 0)
    for b in range(ROWS):
        position = jnp.where(sub == b, length_s[b].astype(F32), position)
        adapter = jnp.where(sub_wide == b, adapter_s[b], adapter)
    chosen = adapter == lax.broadcasted_iota(jnp.int32, adapter.shape, 1) // (2 * RANK)
    angles = position * freq_v[...]
    cosine, sine = jnp.cos(angles), jnp.sin(angles)
    qup_v[:, RANK:, :] = jnp.zeros((ADAPTERS, RANK, HALF), BF16)
    vup_v[:, :RANK, :] = jnp.zeros((ADAPTERS, RANK, HEAD_SIZE), BF16)

    landed(0, z_buf.at[pl.ds(0, NZ * NC - 1)])
    tiles = [z_buf[2 * k].astype(F32) + z_buf[2 * k + 1].astype(F32) for k in range(NZ)]
    packed = [jnp.concatenate([tiles[k][:ROWS], tiles[k + 1][:ROWS]], axis=0) for k in range(0, NZ, 2)]
    gain_rows = jnp.zeros((2 * ROWS, 128), F32)
    sub2 = lax.broadcasted_iota(jnp.int32, gain_rows.shape, 0)
    for k in range(NZ):
        gain_rows = jnp.where(sub2 == k, tiles[k][ROWS : ROWS + 1], gain_rows)
    here = x * NY + y
    xy_mine = xy_buf.at[here]
    sq_mine = sq_buf.at[here]
    sq_mine[...] = added([tile[:ROWS] * tile[:ROWS] for tile in tiles])
    for o in XY_PARTNERS:
        send(1, o, sq_mine, sq_mine)
    xy_mine[...] = jnp.concatenate(packed + [gain_rows], axis=0).astype(BF16)
    for ky in range(NY):
        to_y = lax.rem(x + ky, NY)
        for kx in (2, 1, 3, 0):
            there = at_seq[kx][0], to_y * NC + c

            def block_to():
                send_to(7, there, xy_mine, xy_mine, xy_sem.at[here])

            if kx == 0:
                pl.when(to_y != y)(block_to)
            else:
                block_to()
    sent.append((7, xy_buf.at[pl.ds(0, NX * NY - 1)]))

    def arrived(k):
        pltpu.make_async_copy(xy_buf.at[k], xy_buf.at[k], xy_sem.at[k]).wait()

    landed(1, sq_buf.at[pl.ds(0, NX * NY - 1)])
    square_sum = jnp.sum(added([sq_buf[k] for k in range(NX * NY)]), axis=1, keepdims=True)
    scaling = jnp.broadcast_to(lax.rsqrt(square_sum / MODEL_WIDTH + EPSILON), (ROWS, 128))
    scaling = jnp.concatenate([scaling, scaling], axis=0)

    for ky in range(NY):
        pl.when(y * NY + ky != here)(lambda ky=ky: arrived(y * NY + ky))
    for ky in range(NY):
        k = y * NY + ky
        gain_k = xy_buf[k, pl.ds(NZ * ROWS, 2 * ROWS)].astype(F32)
        gain_k = jnp.where(c == 0, gain_k[:4], gain_k[4:8])
        for p in range(2):
            start = pl.multiple_of(c * 4 * ROWS + p * 2 * ROWS, 2 * ROWS)
            part = xy_buf[k, pl.ds(start, 2 * ROWS)].astype(F32) * scaling
            for i in range(2):
                tile = (2 * p + i) * NY + ky
                one = part[i * ROWS : (i + 1) * ROWS] * gain_k[2 * p + i : 2 * p + i + 1]
                group_in[:, pl.ds(tile * 128, 128)] = one.astype(BF16)
    fetches["down"].wait()
    low_width = MODEL_WIDTH // GROUPS
    b_mine = b_buf.at[head]
    b_mine[...] = lax.dot_general(
        group_in[...], down_v[...].reshape(ADAPTERS * 2 * RANK, low_width), NT, preferred_element_type=F32
    )
    for o in HEAD_PARTNERS:
        send(2, o, b_mine, b_mine)

    for k in range(NX * NY):
        pl.when((k // NY != y) & (k != here))(lambda k=k: arrived(k))
    for k in range(NX * NY):
        kx, ky = k // NY, k % NY
        gain_k = xy_buf[k, pl.ds(NZ * ROWS, 2 * ROWS)].astype(F32)
        for p in range(NZ // 2):
            part = xy_buf[k, pl.ds(2 * ROWS * p, 2 * ROWS)].astype(F32) * scaling
            for i in range(2):
                kz = 2 * p + i
                tile = (kx * NZ + kz) * NY + ky
                normed[:, pl.ds(tile * 128, 128)] = (part[i * ROWS : (i + 1) * ROWS] * gain_k[kz : kz + 1]).astype(BF16)

    fetches["kvw"].wait()
    seq_width = MODEL_WIDTH // SEQ
    keyval_part = jnp.dot(
        normed[:, pl.ds(pl.multiple_of(seq * seq_width, seq_width), seq_width)], kvw_v[...], preferred_element_type=F32
    )
    fetches["qw"].wait()
    query_plain = lax.dot_general(normed[...], qw_v[...], NT, preferred_element_type=F32)
    for k in range(4):
        c_msg[k] = jnp.concatenate([query_plain, keyval_part[:, k * HALF : (k + 1) * HALF]], axis=1)
    fetches["qup"].wait()
    fetches["vup"].wait()

    landed(2, b_buf.at[pl.ds(0, GROUPS - 1)])
    low_sum = added([b_buf[k] for k in range(GROUPS)])
    low_rank = jnp.where(chosen, low_sum, 0.0).astype(BF16)
    query_delta = jnp.dot(
        low_rank, qup_v[...].reshape(ADAPTERS * 2 * RANK, HALF), preferred_element_type=F32
    )
    for k in range(4):
        c_msg[k, :, pl.ds(0, HALF)] = (c_msg[k, :, pl.ds(0, HALF)] + query_delta).astype(BF16).astype(F32)
    c_buf[pl.ds(seq, 1)] = c_msg[pl.ds(lax.rem(z, 4), 1)]
    for o in SEQ_PARTNERS:
        send(3, o, c_msg.at[lax.rem(z + o[2], 4)], c_buf.at[seq])
    value_delta = jnp.dot(
        low_rank, vup_v[...].reshape(ADAPTERS * 2 * RANK, HEAD_SIZE), preferred_element_type=F32
    )

    landed(3, c_buf.at[pl.ds(0, SEQ - 1)])
    kv_rows[...] = added([c_buf[k] for k in range(SEQ)])
    kv_piece = jnp.broadcast_to(kv_rows[pl.ds(seq // QUADS, 1)], (HEADS, 128))
    halves = [(c_buf[2 * h], c_buf[2 * h + 1]) for h in range(HEADS)]
    first = [former * cosine - latter * sine for former, latter in halves]
    second = [latter * cosine + former * sine for former, latter in halves]
    turned = [jnp.concatenate([first[h][:, :HALF], second[h][:, :HALF]], axis=1) for h in range(HEADS)]
    for h in range(HEADS):
        q_rot[pl.ds(h * ROWS, ROWS)] = turned[h].astype(BF16).astype(F32)

    fetches["k"].wait()
    fetches["v"].wait()
    where = seq * SPAN + lax.broadcasted_iota(jnp.int32, (HEADS, SPAN), 1)
    lane_h = lax.broadcasted_iota(jnp.int32, (HEADS, 128), 1)
    rows = [lax.rem(2 * x + k, ROWS) for k in (4, 5, 2, 3, 6, 7, 0, 1)]
    queries = [q_rot[pl.ds(b, HEADS, stride=ROWS)].astype(BF16) for b in rows]
    own = pl.ds(pl.multiple_of(seq * 8, 8), 8)
    parts = ((range(0, 2), (2,)), (range(2, 6), (1, 3)), (range(6, 8), (0,)))
    scores = {}

    def score(some):
        for i in some:
            scores[i] = lax.dot_general(queries[i], k_v[rows[i]], NT, preferred_element_type=F32)

    score(parts[0][0])
    for n, (some, turns) in enumerate(parts):
        if n + 1 < len(parts):
            score(parts[n + 1][0])
        valid = {i: where < length_s[rows[i]] for i in some}
        masked = {i: jnp.where(valid[i], scores[i] * SCORE_SCALE, MASKED) for i in some}
        block_max = {i: jnp.max(masked[i], axis=1, keepdims=True) for i in some}
        weights = {i: jnp.where(valid[i], jnp.exp(masked[i] - block_max[i]), 0.0) for i in some}
        block_total = {i: jnp.sum(weights[i], axis=1, keepdims=True) for i in some}
        block_acc = {i: jnp.dot(weights[i].astype(BF16), v_v[rows[i]], preferred_element_type=F32) for i in some}
        for i in some:
            facts = jnp.where(lane_h < 32, block_max[i], jnp.where(lane_h < 64, block_total[i], kv_piece))
            for k in range(QUADS):
                d_msg[rows[i] * QUADS + k, pl.ds(0, 4)] = block_acc[i][4 * k : 4 * k + 4]
                d_msg[rows[i] * QUADS + k, pl.ds(4, 4)] = facts[4 * k : 4 * k + 4]
        for o in SEQ_PARTNERS:
            if o[0] in turns:
                send(4, o, d_msg.at[at_seq[o[0]][o[2]]], d_buf.at[own])
    d_buf[own] = d_msg[pl.ds(seq, 1)].reshape(8, 128)
    landed(4, d_buf.at[pl.ds(0, (SEQ - 1) * 8)])

    quarter = [d_buf[pl.ds(8 * k + 4, ROWS, stride=8 * QUADS)] for k in range(4)]
    key_first = quarter[0] * cosine - quarter[1] * sine
    key_second = quarter[1] * cosine + quarter[0] * sine
    key_new = jnp.concatenate([key_first[:, HALF:], key_second[:, HALF:]], axis=1).astype(BF16)
    value_new = (jnp.concatenate([quarter[2][:, HALF:], quarter[3][:, HALF:]], axis=1) + value_delta).astype(BF16)
    kv_ref[:, pl.ds(0, HEAD_SIZE)] = key_new
    kv_ref[:, pl.ds(HEAD_SIZE, HEAD_SIZE)] = value_new

    row, quad = seq // QUADS, lax.rem(seq, QUADS)
    kv_rows[...] = key_new.astype(F32)
    own_key = kv_rows[pl.ds(row, 1)]
    kv_rows[...] = value_new.astype(F32)
    own_value = kv_rows[pl.ds(row, 1)]
    own_queries = q_rot[pl.ds(quad * 4 * ROWS + row, 4, stride=ROWS)]
    self_score = jnp.sum(own_queries * own_key, axis=1, keepdims=True) * SCORE_SCALE
    four = range(4)
    acc = [d_buf[pl.ds(j, SEQ, stride=8)] for j in four]
    facts = [d_buf[pl.ds(4 + j, SEQ, stride=8)] for j in four]
    peaks = [jnp.broadcast_to(facts[j][:, :1], (SEQ, 128)) for j in four]
    own_score = [jnp.broadcast_to(self_score[j : j + 1], (1, 128)) for j in four]
    highest = [jnp.maximum(jnp.max(peaks[j], axis=0, keepdims=True), own_score[j]) for j in four]
    factor = [jnp.exp(peaks[j] - highest[j]) for j in four]
    self_weight = [jnp.exp(own_score[j] - highest[j]) for j in four]
    summed = [jnp.sum(factor[j] * facts[j], axis=0, keepdims=True) for j in four]
    summed = [jnp.broadcast_to(summed[j][:, 32:33], (1, 128)) + self_weight[j] for j in four]
    weighted = [jnp.sum(factor[j] * acc[j], axis=0, keepdims=True) + self_weight[j] * own_value for j in four]
    e_rows = [weighted[j] / summed[j] for j in four]
    attended_own = jnp.concatenate(e_rows + e_rows, axis=0).astype(BF16).astype(F32)
    e_buf[own] = attended_own
    for o in SEQ_PARTNERS:
        send(5, o, e_buf.at[own], e_buf.at[own])
    fetches["ow"].wait()
    landed(5, e_buf.at[pl.ds(0, (SEQ - 1) * 8)])

    attended = jnp.concatenate(
        [e_buf[pl.ds(8 * (h // 4) + h % 4, ROWS, stride=8 * QUADS)] for h in range(HEADS)], axis=1
    ).astype(BF16)
    partial = jnp.dot(attended, ow_v[...], preferred_element_type=F32)
    for k in range(GROUPS):
        tile = partial[:, 128 * (k // 2) : 128 * (k // 2) + 128]
        if k % 2:
            tile = pltpu.roll(tile, HALF, 1)
        f_msg[k] = tile
    f_buf[pl.ds(head, 1)] = f_msg[pl.ds(head, 1)]
    for o in HEAD_PARTNERS:
        send(6, o, f_msg.at[at_head[o[1]][o[3]]], f_buf.at[head])
    landed(6, f_buf.at[pl.ds(0, GROUPS - 1)])
    total = f_buf[0]
    for k in range(1, GROUPS):
        total = total + f_buf[k]
    out_ref[...] = total[:, :HALF].astype(BF16)
    for phase, ref in sent:
        pltpu.make_async_copy(ref, ref, send_sem.at[phase]).wait()


def write_out(delta_ref, keyval_ref, delta_hbm, keyval_hbm, sem):
    first = pltpu.make_async_copy(delta_ref, delta_hbm, sem.at[0])
    second = pltpu.make_async_copy(keyval_ref, keyval_hbm, sem.at[1])
    first.start()
    second.start()
    first.wait()
    second.wait()


def local(
    residual_input,
    norm_gain_vector,
    query_weight,
    key_value_weight,
    output_weight,
    adapter_down_factors,
    query_up_factors,
    value_up_factors,
    adapter_index,
    lengths,
    rotated_key_cache,
    earlier_value_cache,
):
    with jax.ensure_compile_time_eval():
        frequency = jnp.exp(jnp.arange(HALF, dtype=F32) * (-math.log(ROPE_BASE) / HALF))
        frequency = np.asarray(frequency)
    frequency = jnp.asarray(np.concatenate([frequency, frequency])[None, :])
    operands = (
        residual_input,
        norm_gain_vector,
        jnp.transpose(query_weight, (1, 2, 0)).reshape(HALF, MODEL_WIDTH),
        key_value_weight.reshape(MODEL_WIDTH // SEQ, 2 * HEAD_SIZE),
        output_weight.reshape(HEADS * HEAD_SIZE, MODEL_WIDTH // SEQ),
        jnp.transpose(adapter_down_factors, (0, 2, 1)),
        query_up_factors.reshape(ADAPTERS, RANK, HALF),
        value_up_factors.reshape(ADAPTERS, RANK, HEAD_SIZE),
        adapter_index,
        lengths,
        rotated_key_cache.reshape(ROWS, SPAN, HEAD_SIZE),
        earlier_value_cache.reshape(ROWS, SPAN, HEAD_SIZE),
        frequency,
    )
    dma, vmem = pltpu.SemaphoreType.DMA, pltpu.VMEM
    attn_delta, new_keyval = pl.pallas_call(
        kernel,
        out_shape=(
            jax.ShapeDtypeStruct((ROWS, HALF), BF16),
            jax.ShapeDtypeStruct((ROWS, 2 * HEAD_SIZE), BF16),
        ),
        in_specs=[pl.BlockSpec(memory_space=pl.ANY)] * len(operands),
        out_specs=(pl.BlockSpec(memory_space=vmem), pl.BlockSpec(memory_space=vmem)),
        scratch_shapes=[
            vmem((ROWS, HALF), BF16),
            vmem((HALF,), BF16),
            vmem((HALF, MODEL_WIDTH), BF16),
            vmem((MODEL_WIDTH // SEQ, 2 * HEAD_SIZE), BF16),
            vmem((HEADS * HEAD_SIZE, MODEL_WIDTH // SEQ), BF16),
            vmem((ADAPTERS, 2 * RANK, MODEL_WIDTH // GROUPS), BF16),
            vmem((ADAPTERS, 2 * RANK, HALF), BF16),
            vmem((ADAPTERS, 2 * RANK, HEAD_SIZE), BF16),
            pltpu.SMEM((ADAPTERS,), jnp.int32),
            pltpu.SMEM((ROWS,), jnp.int32),
            vmem((ROWS, SPAN, HEAD_SIZE), BF16),
            vmem((ROWS, SPAN, HEAD_SIZE), BF16),
            vmem((1, 128), F32),
            vmem((2 * ROWS, 128), BF16),
            vmem((NZ * NC, 2 * ROWS, 128), BF16),
            vmem((NX * NY, NZ * ROWS + 2 * ROWS, 128), BF16),
            vmem((NX * NY, ROWS, 128), F32),
            vmem((ROWS, MODEL_WIDTH // GROUPS), BF16),
            vmem((ROWS, MODEL_WIDTH), BF16),
            vmem((GROUPS, ROWS, ADAPTERS * 2 * RANK), F32),
            vmem((4, ROWS, 128), F32),
            vmem((SEQ, ROWS, 128), F32),
            vmem((HEADS * ROWS, 128), F32),
            vmem((SEQ, 8, 128), F32),
            vmem((SEQ * 8, 128), F32),
            vmem((ROWS, 128), F32),
            vmem((SEQ * 8, 128), F32),
            vmem((GROUPS, ROWS, 128), F32),
            vmem((GROUPS, ROWS, 128), F32),
            dma((13,)),
            dma((8,)),
            dma((7,)),
            dma((NX * NY,)),
        ],
        compiler_params=pltpu.CompilerParams(
            collective_id=0, has_side_effects=True, vmem_limit_bytes=62 * 2**20
        ),
        name="decode_attention",
    )(*operands)
    attn_delta, new_keyval = pl.pallas_call(
        write_out,
        out_shape=(
            jax.ShapeDtypeStruct((ROWS, HALF), BF16),
            jax.ShapeDtypeStruct((ROWS, 2 * HEAD_SIZE), BF16),
        ),
        in_specs=[pl.BlockSpec(memory_space=pl.ANY)] * 2,
        out_specs=[pl.BlockSpec(memory_space=pl.ANY)] * 2,
        scratch_shapes=[dma((2,))],
        name="write_out",
    )(attn_delta, new_keyval)
    return attn_delta, new_keyval[:, None, :]


def solution(mesh):
    return jax.shard_map(
        local,
        mesh=mesh,
        in_specs=(
            P(None, ("kvseq", "kvhead")),
            P(("kvseq", "kvhead")),
            P(None, "kvhead", "kvseq"),
            P("kvseq", "kvhead", None),
            P("kvhead", None, "kvseq"),
            P(None, "kvhead", None),
            P(None, None, "kvhead", "kvseq"),
            P(None, None, "kvhead", None),
            P(),
            P(),
            P(None, "kvseq", "kvhead", None),
            P(None, "kvseq", "kvhead", None),
        ),
        out_specs=(P(None, ("kvseq", "kvhead")), P(None, "kvhead", None)),
        check_vma=False,
    )
```

```python
import math

import jax
import jax.numpy as jnp
import numpy as np
from jax import lax
from jax.experimental import pallas as pl
from jax.experimental.pallas import tpu as pltpu
from jax.sharding import PartitionSpec as P

MODEL_WIDTH = 16384
HEADS = 16
HEAD_SIZE = 128
HALF = HEAD_SIZE // 2
ADAPTERS = 8
RANK = 16
ROWS = 8
SPAN = 1024
NX, NY, NZ, NC = 4, 4, 8, 2
SEQ = NX * NZ
GROUPS = NY * NC
QUADS = SEQ // ROWS
GROUP_WIDTH = MODEL_WIDTH // GROUPS

EPSILON = 1e-05
ROPE_BASE = 500000.0
MASKED = -1e30
SCORE_SCALE = 1.0 / math.sqrt(HEAD_SIZE)
MESH = pl.DeviceIdType.MESH
F32 = jnp.float32
BF16 = jnp.bfloat16
NT = (((1,), (1,)), ((), ()))


def ring(k, n):
    return min(k, n - k)


def added(terms):
    while len(terms) > 1:
        terms = [sum(terms[k + 1 : k + 2], terms[k]) for k in range(0, len(terms), 2)]
    return terms[0]


def offsets(xs, ys, zs, cs):
    found = [(x, y, z, c) for x in xs for y in ys for z in zs for c in cs if (x, y, z, c) != (0, 0, 0, 0)]
    return sorted(found, key=lambda o: (-(ring(o[0], NX) + ring(o[1], NY) + ring(o[2], NZ)), -o[3]))


Z_PARTNERS = offsets([0], [0], range(NZ), range(NC))
XY_PARTNERS = offsets(range(NX), range(NY), [0], [0])
HEAD_PARTNERS = offsets([0], range(NY), [0], range(NC))
SEQ_PARTNERS = offsets(range(NX), [0], range(NZ), [0])


def kernel(
    x_hbm, gain_hbm, qw_hbm, kvw_hbm, ow_hbm, down_hbm, qup_hbm, vup_hbm, adapter_hbm, length_hbm, k_hbm, v_hbm, freq_hbm,
    out_ref, kv_ref,
    x_v, gain_v, qw_v, kvw_v, ow_v, down_v, qup_v, vup_v, adapter_s, length_s, k_v, v_v, freq_v,
    z_msg, z_buf, xy_buf, sq_buf, normed, b_buf, c_msg, c_buf, q_rot, d_msg, d_buf, kv_rows, e_buf, f_msg, f_buf,
    local_sem, send_sem, recv_sem, xy_sem,
):
    seq, head = lax.axis_index("kvseq"), lax.axis_index("kvhead")
    x, z = seq // NZ, lax.rem(seq, NZ)
    y, c = head // NC, lax.rem(head, NC)

    at_x = [lax.rem(x + k, NX) for k in range(NX)]
    at_y = [lax.rem(y + k, NY) for k in range(NY)]
    at_z = [lax.rem(z + k, NZ) for k in range(NZ)]
    at_c = [c, 1 - c]
    at_seq = [[at_x[i] * NZ + at_z[k] for k in range(NZ)] for i in range(NX)]
    at_head = [[at_y[i] * NC + at_c[k] for k in range(NC)] for i in range(NY)]

    def place(o):
        return at_seq[o[0]][o[2]], at_head[o[1]][o[3]]

    barrier = pltpu.get_barrier_semaphore()
    for o in XY_PARTNERS + Z_PARTNERS:
        pl.semaphore_signal(barrier, inc=1, device_id=place(o), device_id_type=MESH)

    fetches = {}

    def fetch(name, src, dst):
        fetches[name] = pltpu.make_async_copy(src, dst, local_sem.at[len(fetches)])
        fetches[name].start()

    fetch("x", x_hbm, x_v)
    fetch("gain", gain_hbm, gain_v)
    fetch("length", length_hbm, length_s)
    fetch("adapter", adapter_hbm, adapter_s)
    fetch("freq", freq_hbm, freq_v)

    sent = []

    def send_to(phase, device, src, dst, sem):
        copy = pltpu.make_async_remote_copy(
            src_ref=src, dst_ref=dst, send_sem=send_sem.at[phase], recv_sem=sem, device_id=device, device_id_type=MESH
        )
        copy.start()

    def send(phase, o, src, dst):
        send_to(phase, place(o), src, dst, recv_sem.at[phase])

    def landed(phase, ref):
        pltpu.make_async_copy(ref, ref, recv_sem.at[phase]).wait()
        sent.append((phase, ref))

    lane = lax.broadcasted_iota(jnp.int32, (ROWS, 128), 1)
    sub = lax.broadcasted_iota(jnp.int32, (ROWS, 128), 0)

    fetches["x"].wait()
    fetches["gain"].wait()
    mine = x_v[...].astype(F32)
    gains = jnp.broadcast_to(gain_v[...].astype(F32).reshape(1, HALF), (ROWS, HALF))
    both = jnp.concatenate([mine, jnp.where(sub[:, :HALF] == 0, gains, 0.0)], axis=0)
    both = jnp.concatenate([both, both], axis=1)
    lane2 = lax.broadcasted_iota(jnp.int32, (2 * ROWS, 128), 1)
    block = jnp.where(lane2 // HALF == c, both, 0.0).astype(BF16)
    z_msg[...] = block
    z_buf[pl.ds(z * NC + c, 1)] = block[None]

    pl.semaphore_wait(barrier, len(XY_PARTNERS) + len(Z_PARTNERS))
    for o in Z_PARTNERS:
        send(0, o, z_msg, z_buf.at[z * NC + c])
    fetch("down", down_hbm, down_v)
    fetch("kvw", kvw_hbm, kvw_v)
    fetch("qw", qw_hbm, qw_v)
    fetch("qup", qup_hbm, qup_v.at[:, pl.ds(0, RANK)])
    fetch("vup", vup_hbm, vup_v.at[:, pl.ds(RANK, RANK)])
    fetch("k", k_hbm, k_v)
    fetch("v", v_hbm, v_v)
    fetch("ow", ow_hbm, ow_v)

    fetches["length"].wait()
    fetches["freq"].wait()
    fetches["adapter"].wait()
    position = jnp.zeros((ROWS, 128), F32)
    adapter = jnp.zeros((ROWS, ADAPTERS * 2 * RANK), jnp.int32)
    sub_wide = lax.broadcasted_iota(jnp.int32, adapter.shape, 0)
    for b in range(ROWS):
        position = jnp.where(sub == b, length_s[b].astype(F32), position)
        adapter = jnp.where(sub_wide == b, adapter_s[b], adapter)
    chosen = adapter == lax.broadcasted_iota(jnp.int32, adapter.shape, 1) // (2 * RANK)
    angles = position * freq_v[...]
    cosine, sine = jnp.cos(angles), jnp.sin(angles)
    signed_sine = jnp.where(lane < HALF, -sine, sine)
    qup_v[:, RANK:, :] = jnp.zeros((ADAPTERS, RANK, HALF), BF16)
    vup_v[:, :RANK, :] = jnp.zeros((ADAPTERS, RANK, HEAD_SIZE), BF16)

    landed(0, z_buf.at[pl.ds(0, NZ * NC - 1)])
    tiles = [z_buf[2 * k].astype(F32) + z_buf[2 * k + 1].astype(F32) for k in range(NZ)]
    squares = added([tile[:ROWS] * tile[:ROWS] for tile in tiles])
    facts = squares + pltpu.roll(squares, HALF, 1)
    half = [jnp.where(c == 0, tiles[k], tiles[k + NZ // 2]) for k in range(NZ // 2)]
    for k in range(NZ // 2):
        gain_k = half[k][ROWS : ROWS + 1]
        facts = jnp.where((sub == 2 * k) & (lane >= HALF), pltpu.roll(gain_k, HALF, 1), facts)
        facts = jnp.where((sub == 2 * k + 1) & (lane >= HALF), gain_k, facts)
    here = x * NY + y
    xy_mine = xy_buf.at[here]
    sq_mine = sq_buf.at[here]
    sq_mine[...] = facts
    for o in XY_PARTNERS:
        send(1, o, sq_mine, sq_mine)
    xy_mine[...] = jnp.concatenate([t[:ROWS] for t in half], axis=0).astype(BF16)
    for ky in range(NY):
        to_y = lax.rem(x + ky, NY)
        for kx in (2, 1, 3, 0):
            there = at_seq[kx][0], to_y * NC + c

            def block_to():
                send_to(7, there, xy_mine, xy_mine, xy_sem.at[here])

            if kx == 0:
                pl.when(to_y != y)(block_to)
            else:
                block_to()
    sent.append((7, xy_buf.at[pl.ds(0, NX * NY - 1)]))

    def arrived(k):
        pltpu.make_async_copy(xy_buf.at[k], xy_buf.at[k], xy_sem.at[k]).wait()

    landed(1, sq_buf.at[pl.ds(0, NX * NY - 1)])
    square_sum = added([sq_buf[k] for k in range(NX * NY)])
    square_sum = jnp.sum(jnp.where(lane < HALF, square_sum, 0.0), axis=1, keepdims=True)
    scaling = jnp.broadcast_to(lax.rsqrt(square_sum / MODEL_WIDTH + EPSILON), (ROWS, 128))
    scaling = jnp.concatenate([scaling, scaling], axis=0)

    def normalize(kx):
        for ky in range(NY):
            pl.when(kx * NY + ky != here)(lambda ky=ky: arrived(kx * NY + ky))
        group = kx * NC + c
        for ky in range(NY):
            k = kx * NY + ky
            gain_odd = sq_buf[k]
            gain_even = pltpu.roll(gain_odd, HALF, 1)
            for p in range(2):
                part = xy_buf[k, pl.ds(p * 2 * ROWS, 2 * ROWS)].astype(F32) * scaling
                for i in range(2):
                    n = 2 * p + i
                    gain_row = jnp.where(lane[:1] < HALF, gain_even[2 * n : 2 * n + 1], gain_odd[2 * n + 1 : 2 * n + 2])
                    one = part[i * ROWS : (i + 1) * ROWS] * gain_row
                    normed[group, :, pl.ds((n * NY + ky) * 128, 128)] = one.astype(BF16)

    normalize(y)
    fetches["down"].wait()
    b_mine = b_buf.at[head]
    b_mine[...] = lax.dot_general(
        normed[head], down_v[...].reshape(ADAPTERS * 2 * RANK, GROUP_WIDTH), NT, preferred_element_type=F32
    )
    for o in HEAD_PARTNERS:
        send(2, o, b_mine, b_mine)

    other = (0, 0, 0, 1)
    send(8, other, normed.at[head], normed.at[head])
    for k in range(1, NX):
        normalize(at_y[k])
        group = at_y[k] * NC + c
        send(8, other, normed.at[group], normed.at[group])

    def project(group):
        weight = qw_v[:, pl.ds(pl.multiple_of(group * GROUP_WIDTH, GROUP_WIDTH), GROUP_WIDTH)]
        return lax.dot_general(normed[group], weight, NT, preferred_element_type=F32)

    fetches["qw"].wait()
    fetches["qup"].wait()
    fetches["vup"].wait()
    fetches["kvw"].wait()
    query_own = added([project(k * NC + c) for k in range(NX)])
    c_msg[0, :, pl.ds(0, HALF)] = query_own
    query_up = qup_v[...].reshape(ADAPTERS * 2 * RANK, HALF)
    query_up = jnp.concatenate([query_up, query_up], axis=1)
    landed(8, normed.at[pl.ds(0, NX)])
    query_plain = added([project(k * NC + 1 - c) for k in range(NX)]) + c_msg[0, :, pl.ds(0, HALF)]
    seq_width = MODEL_WIDTH // SEQ
    seq_start = pl.multiple_of(lax.rem(z, 4) * seq_width, seq_width)
    keyval_part = jnp.dot(
        normed[x * NC + z // 4, :, pl.ds(seq_start, seq_width)], kvw_v[...], preferred_element_type=F32
    )
    query_lanes = lane // HALF == lax.rem(z, 2)
    plain = jnp.concatenate([query_plain, query_plain], axis=1)
    for k in range(4):
        quarter = keyval_part[:, k * HALF : (k + 1) * HALF]
        c_msg[k] = jnp.where(query_lanes, plain, jnp.concatenate([quarter, quarter], axis=1))

    landed(2, b_buf.at[pl.ds(0, GROUPS - 1)])
    low_sum = added([b_buf[k] for k in range(GROUPS)])
    low_rank = jnp.where(chosen, low_sum, 0.0).astype(BF16)
    query_delta = jnp.dot(low_rank, query_up, preferred_element_type=F32)
    for k in range(4):
        message = c_msg[k]
        c_msg[k] = jnp.where(query_lanes, (message + query_delta).astype(BF16).astype(F32), message)
    c_buf[pl.ds(seq, 1)] = c_msg[pl.ds(lax.rem(z, 4), 1)]
    for o in SEQ_PARTNERS:
        send(3, o, c_msg.at[lax.rem(z + o[2], 4)], c_buf.at[seq])
    value_delta = jnp.dot(
        low_rank, vup_v[...].reshape(ADAPTERS * 2 * RANK, HEAD_SIZE), preferred_element_type=F32
    )

    landed(3, c_buf.at[pl.ds(0, SEQ - 1)])
    pairs = [(c_buf[2 * h], c_buf[2 * h + 1]) for h in range(HEADS)]
    whole = [jnp.where(lane < HALF, even, odd) for even, odd in pairs]
    turned = [t * cosine + pltpu.roll(t, HALF, 1) * signed_sine for t in whole]
    for h in range(HEADS):
        q_rot[pl.ds(h * ROWS, ROWS)] = turned[h].astype(BF16).astype(F32)
    kv_rows[...] = added([even for even, _ in pairs]) + pltpu.roll(added([odd for _, odd in pairs]), HALF, 1)
    kv_piece = jnp.broadcast_to(kv_rows[pl.ds(seq // QUADS, 1)], (HEADS, 128))

    fetches["k"].wait()
    fetches["v"].wait()
    where = seq * SPAN + lax.broadcasted_iota(jnp.int32, (HEADS, SPAN), 1)
    lane_h = lax.broadcasted_iota(jnp.int32, (HEADS, 128), 1)
    rows = [lax.rem(2 * x + k, ROWS) for k in (4, 5, 2, 3, 6, 7, 0, 1)]
    queries = [q_rot[pl.ds(b, HEADS, stride=ROWS)].astype(BF16) for b in rows]
    own = pl.ds(pl.multiple_of(seq * 8, 8), 8)
    parts = ((range(0, 2), (2,)), (range(2, 6), (1, 3)), (range(6, 8), (0,)))
    scores = {}

    def score(some):
        for i in some:
            scores[i] = lax.dot_general(queries[i], k_v[rows[i]], NT, preferred_element_type=F32)

    score(parts[0][0])
    for n, (some, turns) in enumerate(parts):
        if n + 1 < len(parts):
            score(parts[n + 1][0])
        valid = {i: where < length_s[rows[i]] for i in some}
        masked = {i: jnp.where(valid[i], scores[i] * SCORE_SCALE, MASKED) for i in some}
        block_max = {i: jnp.max(masked[i], axis=1, keepdims=True) for i in some}
        weights = {i: jnp.where(valid[i], jnp.exp(masked[i] - block_max[i]), 0.0) for i in some}
        block_total = {i: jnp.sum(weights[i], axis=1, keepdims=True) for i in some}
        block_acc = {i: jnp.dot(weights[i].astype(BF16), v_v[rows[i]], preferred_element_type=F32) for i in some}
        for i in some:
            facts = jnp.where(lane_h < 32, block_max[i], jnp.where(lane_h < 64, block_total[i], kv_piece))
            for k in range(2):
                heads = block_acc[i][8 * k : 8 * k + 8]
                about = pltpu.roll(facts[8 * k : 8 * k + 8], 4, 0)
                d_msg[rows[i] * QUADS + 2 * k] = jnp.where(sub < 4, heads, about)
                d_msg[rows[i] * QUADS + 2 * k + 1] = jnp.where(sub < 4, about, heads)
        for o in SEQ_PARTNERS:
            if o[0] in turns:
                send(4, o, d_msg.at[at_seq[o[0]][o[2]]], d_buf.at[own])
    d_buf[own] = d_msg[pl.ds(seq, 1)].reshape(8, 128)
    landed(4, d_buf.at[pl.ds(0, (SEQ - 1) * 8)])

    row, quad = seq // QUADS, lax.rem(seq, QUADS)
    acc_row = lax.rem(quad, 2) * 4
    facts_row = 4 - acc_row
    quarter = [d_buf[pl.ds(8 * k + facts_row, ROWS, stride=8 * QUADS)] for k in range(4)]
    key_first = quarter[0] * cosine - quarter[1] * sine
    key_second = quarter[1] * cosine + quarter[0] * sine
    key_new = jnp.concatenate([key_first[:, HALF:], key_second[:, HALF:]], axis=1).astype(BF16)
    value_new = (jnp.concatenate([quarter[2][:, HALF:], quarter[3][:, HALF:]], axis=1) + value_delta).astype(BF16)
    kv_ref[:, pl.ds(0, HEAD_SIZE)] = key_new
    kv_ref[:, pl.ds(HEAD_SIZE, HEAD_SIZE)] = value_new

    kv_rows[...] = key_new.astype(F32)
    own_key = kv_rows[pl.ds(row, 1)]
    kv_rows[...] = value_new.astype(F32)
    own_value = kv_rows[pl.ds(row, 1)]
    own_queries = q_rot[pl.ds(quad * 4 * ROWS + row, 4, stride=ROWS)]
    self_score = jnp.sum(own_queries * own_key, axis=1, keepdims=True) * SCORE_SCALE
    four = range(4)
    acc = [d_buf[pl.ds(acc_row + j, SEQ, stride=8)] for j in four]
    facts = [d_buf[pl.ds(facts_row + j, SEQ, stride=8)] for j in four]
    peaks = [jnp.broadcast_to(facts[j][:, :1], (SEQ, 128)) for j in four]
    own_score = [jnp.broadcast_to(self_score[j : j + 1], (1, 128)) for j in four]
    highest = [jnp.maximum(jnp.max(peaks[j], axis=0, keepdims=True), own_score[j]) for j in four]
    factor = [jnp.exp(peaks[j] - highest[j]) for j in four]
    self_weight = [jnp.exp(own_score[j] - highest[j]) for j in four]
    summed = [jnp.sum(factor[j] * facts[j], axis=0, keepdims=True) for j in four]
    summed = [jnp.broadcast_to(summed[j][:, 32:33], (1, 128)) + self_weight[j] for j in four]
    weighted = [jnp.sum(factor[j] * acc[j], axis=0, keepdims=True) + self_weight[j] * own_value for j in four]
    e_rows = [weighted[j] / summed[j] for j in four]
    attended_own = jnp.concatenate(e_rows + e_rows, axis=0).astype(BF16).astype(F32)
    e_buf[own] = attended_own
    for o in SEQ_PARTNERS:
        send(5, o, e_buf.at[own], e_buf.at[own])
    fetches["ow"].wait()
    landed(5, e_buf.at[pl.ds(0, (SEQ - 1) * 8)])

    attended = jnp.concatenate(
        [e_buf[pl.ds(8 * (h // 4) + h % 4, ROWS, stride=8 * QUADS)] for h in range(HEADS)], axis=1
    ).astype(BF16)
    partial = jnp.dot(attended, ow_v[...], preferred_element_type=F32)
    for k in range(GROUPS):
        tile = partial[:, 128 * (k // 2) : 128 * (k // 2) + 128]
        if k % 2:
            tile = pltpu.roll(tile, HALF, 1)
        f_msg[k] = tile
    f_buf[pl.ds(head, 1)] = f_msg[pl.ds(head, 1)]
    for o in HEAD_PARTNERS:
        send(6, o, f_msg.at[at_head[o[1]][o[3]]], f_buf.at[head])
    landed(6, f_buf.at[pl.ds(0, GROUPS - 1)])
    total = f_buf[0]
    for k in range(1, GROUPS):
        total = total + f_buf[k]
    out_ref[...] = total[:, :HALF].astype(BF16)
    for phase, ref in sent:
        pltpu.make_async_copy(ref, ref, send_sem.at[phase]).wait()


def write_out(delta_ref, keyval_ref, delta_hbm, keyval_hbm, sem):
    first = pltpu.make_async_copy(delta_ref, delta_hbm, sem.at[0])
    second = pltpu.make_async_copy(keyval_ref, keyval_hbm, sem.at[1])
    first.start()
    second.start()
    first.wait()
    second.wait()


def local(
    residual_input,
    norm_gain_vector,
    query_weight,
    key_value_weight,
    output_weight,
    adapter_down_factors,
    query_up_factors,
    value_up_factors,
    adapter_index,
    lengths,
    rotated_key_cache,
    earlier_value_cache,
):
    with jax.ensure_compile_time_eval():
        frequency = jnp.exp(jnp.arange(HALF, dtype=F32) * (-math.log(ROPE_BASE) / HALF))
        frequency = np.asarray(frequency)
    frequency = jnp.asarray(np.concatenate([frequency, frequency])[None, :])
    operands = (
        residual_input,
        norm_gain_vector,
        jnp.transpose(query_weight, (1, 2, 0)).reshape(HALF, MODEL_WIDTH),
        key_value_weight.reshape(MODEL_WIDTH // SEQ, 2 * HEAD_SIZE),
        output_weight.reshape(HEADS * HEAD_SIZE, MODEL_WIDTH // SEQ),
        jnp.transpose(adapter_down_factors, (0, 2, 1)),
        query_up_factors.reshape(ADAPTERS, RANK, HALF),
        value_up_factors.reshape(ADAPTERS, RANK, HEAD_SIZE),
        adapter_index,
        lengths,
        rotated_key_cache.reshape(ROWS, SPAN, HEAD_SIZE),
        earlier_value_cache.reshape(ROWS, SPAN, HEAD_SIZE),
        frequency,
    )
    dma, vmem = pltpu.SemaphoreType.DMA, pltpu.VMEM
    attn_delta, new_keyval = pl.pallas_call(
        kernel,
        out_shape=(vmem((ROWS, HALF), BF16), vmem((ROWS, 2 * HEAD_SIZE), BF16)),
        in_specs=[pl.BlockSpec(memory_space=pl.ANY)] * len(operands),
        out_specs=(pl.BlockSpec(memory_space=vmem), pl.BlockSpec(memory_space=vmem)),
        scratch_shapes=[
            vmem((ROWS, HALF), BF16),
            vmem((HALF,), BF16),
            vmem((HALF, MODEL_WIDTH), BF16),
            vmem((MODEL_WIDTH // SEQ, 2 * HEAD_SIZE), BF16),
            vmem((HEADS * HEAD_SIZE, MODEL_WIDTH // SEQ), BF16),
            vmem((ADAPTERS, 2 * RANK, MODEL_WIDTH // GROUPS), BF16),
            vmem((ADAPTERS, 2 * RANK, HALF), BF16),
            vmem((ADAPTERS, 2 * RANK, HEAD_SIZE), BF16),
            pltpu.SMEM((ADAPTERS,), jnp.int32),
            pltpu.SMEM((ROWS,), jnp.int32),
            vmem((ROWS, SPAN, HEAD_SIZE), BF16),
            vmem((ROWS, SPAN, HEAD_SIZE), BF16),
            vmem((1, 128), F32),
            vmem((2 * ROWS, 128), BF16),
            vmem((NZ * NC, 2 * ROWS, 128), BF16),
            vmem((NX * NY, NZ // 2 * ROWS, 128), BF16),
            vmem((NX * NY, ROWS, 128), F32),
            vmem((GROUPS, ROWS, GROUP_WIDTH), BF16),
            vmem((GROUPS, ROWS, ADAPTERS * 2 * RANK), F32),
            vmem((4, ROWS, 128), F32),
            vmem((SEQ, ROWS, 128), F32),
            vmem((HEADS * ROWS, 128), F32),
            vmem((SEQ, 8, 128), F32),
            vmem((SEQ * 8, 128), F32),
            vmem((ROWS, 128), F32),
            vmem((SEQ * 8, 128), F32),
            vmem((GROUPS, ROWS, 128), F32),
            vmem((GROUPS, ROWS, 128), F32),
            dma((13,)),
            dma((9,)),
            dma((9,)),
            dma((NX * NY,)),
        ],
        compiler_params=pltpu.CompilerParams(
            collective_id=0, has_side_effects=True, vmem_limit_bytes=62 * 2**20
        ),
        name="decode_attention",
    )(*operands)
    attn_delta, new_keyval = pl.pallas_call(
        write_out,
        out_shape=(
            jax.ShapeDtypeStruct((ROWS, HALF), BF16),
            jax.ShapeDtypeStruct((ROWS, 2 * HEAD_SIZE), BF16),
        ),
        in_specs=[pl.BlockSpec(memory_space=vmem)] * 2,
        out_specs=[pl.BlockSpec(memory_space=pl.ANY)] * 2,
        scratch_shapes=[dma((2,))],
        compiler_params=pltpu.CompilerParams(vmem_limit_bytes=2**20),
        name="write_out",
    )(attn_delta, new_keyval)
    return attn_delta, new_keyval[:, None, :]


def solution(mesh):
    return jax.shard_map(
        local,
        mesh=mesh,
        in_specs=(
            P(None, ("kvseq", "kvhead")),
            P(("kvseq", "kvhead")),
            P(None, "kvhead", "kvseq"),
            P("kvseq", "kvhead", None),
            P("kvhead", None, "kvseq"),
            P(None, "kvhead", None),
            P(None, None, "kvhead", "kvseq"),
            P(None, None, "kvhead", None),
            P(),
            P(),
            P(None, "kvseq", "kvhead", None),
            P(None, "kvseq", "kvhead", None),
        ),
        out_specs=(P(None, ("kvseq", "kvhead")), P(None, "kvhead", None)),
        check_vma=False,
    )
```

```python
import math

import jax
import jax.numpy as jnp
import numpy as np
from jax import lax
from jax.experimental import pallas as pl
from jax.experimental.pallas import tpu as pltpu
from jax.sharding import PartitionSpec as P

MODEL_WIDTH = 16384
HEADS = 16
HEAD_SIZE = 128
HALF = HEAD_SIZE // 2
ADAPTERS = 8
RANK = 16
ROWS = 8
SPAN = 1024
NX, NY, NZ, NC = 4, 4, 8, 2
SEQ = NX * NZ
GROUPS = NY * NC
QUADS = SEQ // ROWS
GROUP_WIDTH = MODEL_WIDTH // GROUPS

EPSILON = 1e-05
ROPE_BASE = 500000.0
MASKED = -1e30
SCORE_SCALE = 1.0 / math.sqrt(HEAD_SIZE)
MESH = pl.DeviceIdType.MESH
F32 = jnp.float32
BF16 = jnp.bfloat16
NT = (((1,), (1,)), ((), ()))


def ring(k, n):
    return min(k, n - k)


def added(terms):
    while len(terms) > 1:
        terms = [sum(terms[k + 1 : k + 2], terms[k]) for k in range(0, len(terms), 2)]
    return terms[0]


def offsets(xs, ys, zs, cs):
    found = [(x, y, z, c) for x in xs for y in ys for z in zs for c in cs if (x, y, z, c) != (0, 0, 0, 0)]
    return sorted(found, key=lambda o: (-(ring(o[0], NX) + ring(o[1], NY) + ring(o[2], NZ)), -o[3]))


Z_PARTNERS = offsets([0], [0], range(NZ), range(NC))
XY_PARTNERS = offsets(range(NX), range(NY), [0], [0])
HEAD_PARTNERS = offsets([0], range(NY), [0], range(NC))
SEQ_PARTNERS = offsets(range(NX), [0], range(NZ), [0])


def kernel(
    x_hbm, gain_hbm, qw_hbm, kvw_hbm, ow_hbm, down_hbm, qup_hbm, vup_hbm, adapter_hbm, length_hbm, k_hbm, v_hbm, freq_hbm,
    out_ref, kv_ref,
    x_v, gain_v, qw_v, kvw_v, ow_v, down_v, qup_v, vup_v, adapter_s, length_s, k_v, v_v, freq_v,
    z_msg, z_buf, xy_buf, sq_buf, normed, b_buf, c_msg, c_buf, up_buf, query_delta, q_rot, d_msg, d_buf, kv_rows, e_buf, f_msg, f_buf,
    local_sem, send_sem, recv_sem, xy_sem, half_sem,
):
    seq, head = lax.axis_index("kvseq"), lax.axis_index("kvhead")
    x, z = seq // NZ, lax.rem(seq, NZ)
    y, c = head // NC, lax.rem(head, NC)

    at_x = [lax.rem(x + k, NX) for k in range(NX)]
    at_y = [lax.rem(y + k, NY) for k in range(NY)]
    at_z = [lax.rem(z + k, NZ) for k in range(NZ)]
    at_c = [c, 1 - c]
    at_seq = [[at_x[i] * NZ + at_z[k] for k in range(NZ)] for i in range(NX)]
    at_head = [[at_y[i] * NC + at_c[k] for k in range(NC)] for i in range(NY)]

    def place(o):
        return at_seq[o[0]][o[2]], at_head[o[1]][o[3]]

    barrier = pltpu.get_barrier_semaphore()
    for o in XY_PARTNERS + Z_PARTNERS:
        pl.semaphore_signal(barrier, inc=1, device_id=place(o), device_id_type=MESH)

    fetches = {}

    def fetch(name, src, dst):
        fetches[name] = pltpu.make_async_copy(src, dst, local_sem.at[len(fetches)])
        fetches[name].start()

    fetch("x", x_hbm, x_v)
    fetch("gain", gain_hbm, gain_v)
    fetch("length", length_hbm, length_s)
    fetch("adapter", adapter_hbm, adapter_s)
    fetch("freq", freq_hbm, freq_v)
    fetch("qup", qup_hbm, qup_v)

    sent = []

    def send_to(phase, device, src, dst, sem):
        copy = pltpu.make_async_remote_copy(
            src_ref=src, dst_ref=dst, send_sem=send_sem.at[phase], recv_sem=sem, device_id=device, device_id_type=MESH
        )
        copy.start()

    def send(phase, o, src, dst):
        send_to(phase, place(o), src, dst, recv_sem.at[phase])

    def landed(phase, ref):
        pltpu.make_async_copy(ref, ref, recv_sem.at[phase]).wait()
        sent.append((phase, ref))

    lane = lax.broadcasted_iota(jnp.int32, (ROWS, 128), 1)
    sub = lax.broadcasted_iota(jnp.int32, (ROWS, 128), 0)

    fetches["x"].wait()
    fetches["gain"].wait()
    mine = x_v[...].astype(F32)
    gains = jnp.broadcast_to(gain_v[...].astype(F32).reshape(1, HALF), (ROWS, HALF))
    both = jnp.concatenate([mine, jnp.where(sub[:, :HALF] == 0, gains, 0.0)], axis=0)
    both = jnp.concatenate([both, both], axis=1)
    lane2 = lax.broadcasted_iota(jnp.int32, (2 * ROWS, 128), 1)
    block = jnp.where(lane2 // HALF == c, both, 0.0).astype(BF16)
    z_msg[...] = block
    z_buf[pl.ds(z * NC + c, 1)] = block[None]

    pl.semaphore_wait(barrier, len(XY_PARTNERS) + len(Z_PARTNERS))
    for o in Z_PARTNERS:
        send(0, o, z_msg, z_buf.at[z * NC + c])
    fetch("down", down_hbm, down_v)
    fetch("kvw", kvw_hbm, kvw_v)
    fetch("qw", qw_hbm, qw_v)
    fetch("vup", vup_hbm, vup_v)
    fetch("k", k_hbm, k_v)
    fetch("v", v_hbm, v_v)
    fetch("ow", ow_hbm, ow_v)

    fetches["length"].wait()
    fetches["freq"].wait()
    fetches["adapter"].wait()
    position = jnp.zeros((ROWS, 128), F32)
    adapter = jnp.zeros((ROWS, ADAPTERS * 2 * RANK), jnp.int32)
    sub_wide = lax.broadcasted_iota(jnp.int32, adapter.shape, 0)
    for b in range(ROWS):
        position = jnp.where(sub == b, length_s[b].astype(F32), position)
        adapter = jnp.where(sub_wide == b, adapter_s[b], adapter)
    chosen = adapter == lax.rem(lax.broadcasted_iota(jnp.int32, adapter.shape, 1), ADAPTERS * RANK) // RANK
    angles = position * freq_v[...]
    cosine, sine = jnp.cos(angles), jnp.sin(angles)
    signed_sine = jnp.where(lane < HALF, -sine, sine)

    landed(0, z_buf.at[pl.ds(0, NZ * NC - 1)])
    tiles = [z_buf[2 * k].astype(F32) + z_buf[2 * k + 1].astype(F32) for k in range(NZ)]
    squares = added([tile[:ROWS] * tile[:ROWS] for tile in tiles])
    facts = squares + pltpu.roll(squares, HALF, 1)
    half = [jnp.where(c == 0, tiles[k], tiles[k + NZ // 2]) for k in range(NZ // 2)]
    for k in range(NZ // 2):
        gain_k = half[k][ROWS : ROWS + 1]
        facts = jnp.where((sub == 2 * k) & (lane >= HALF), pltpu.roll(gain_k, HALF, 1), facts)
        facts = jnp.where((sub == 2 * k + 1) & (lane >= HALF), gain_k, facts)
    here = x * NY + y
    xy_mine = xy_buf.at[here]
    sq_mine = sq_buf.at[here]
    sq_mine[...] = facts
    for o in XY_PARTNERS:
        send(1, o, sq_mine, sq_mine)
    xy_mine[...] = jnp.concatenate([t[:ROWS] for t in half], axis=0).astype(BF16)
    for ky in range(NY):
        to_y = lax.rem(x + ky, NY)
        for kx in (2, 1, 3, 0):
            there = at_seq[kx][0], to_y * NC + c

            def block_to():
                send_to(7, there, xy_mine, xy_mine, xy_sem.at[here])

            if kx == 0:
                pl.when(to_y != y)(block_to)
            else:
                block_to()
    sent.append((7, xy_buf.at[pl.ds(0, NX * NY - 1)]))

    fetches["qup"].wait()
    query_up = qup_v[...].reshape(ADAPTERS * RANK, HALF)
    up_buf[z] = jnp.concatenate([query_up[: ADAPTERS * RANK // 2], query_up[ADAPTERS * RANK // 2 :]], axis=1)
    for o in Z_PARTNERS:
        if o[3] == 0:
            send(9, o, up_buf.at[z], up_buf.at[z])

    def arrived(k):
        pltpu.make_async_copy(xy_buf.at[k], xy_buf.at[k], xy_sem.at[k]).wait()

    landed(1, sq_buf.at[pl.ds(0, NX * NY - 1)])
    square_sum = added([sq_buf[k] for k in range(NX * NY)])
    square_sum = jnp.sum(jnp.where(lane < HALF, square_sum, 0.0), axis=1, keepdims=True)
    scaling = jnp.broadcast_to(lax.rsqrt(square_sum / MODEL_WIDTH + EPSILON), (ROWS, 128))
    scaling = jnp.concatenate([scaling, scaling], axis=0)

    def normalize(kx):
        for ky in range(NY):
            pl.when(kx * NY + ky != here)(lambda ky=ky: arrived(kx * NY + ky))
        group = kx * NC + c
        for ky in range(NY):
            k = kx * NY + ky
            gain_odd = sq_buf[k]
            gain_even = pltpu.roll(gain_odd, HALF, 1)
            for p in range(2):
                part = xy_buf[k, pl.ds(p * 2 * ROWS, 2 * ROWS)].astype(F32) * scaling
                for i in range(2):
                    n = 2 * p + i
                    gain_row = jnp.where(lane[:1] < HALF, gain_even[2 * n : 2 * n + 1], gain_odd[2 * n + 1 : 2 * n + 2])
                    one = part[i * ROWS : (i + 1) * ROWS] * gain_row
                    normed[group, :, pl.ds((n * NY + ky) * 128, 128)] = one.astype(BF16)

    other = (0, 0, 0, 1)
    for k in range(NX):
        normalize(at_y[k])
        group = at_y[k] * NC + c
        send_to(8, place(other), normed.at[group], normed.at[group], half_sem.at[k])
    sent.append((8, normed.at[pl.ds(0, NX)]))

    fetches["down"].wait()
    b_mine = b_buf.at[head]
    for k in range(2):
        factors = down_v[:, k * RANK : (k + 1) * RANK].reshape(ADAPTERS * RANK, GROUP_WIDTH)
        b_mine[:, pl.ds(k * 128, 128)] = lax.dot_general(normed[head], factors, NT, preferred_element_type=F32)
    for o in HEAD_PARTNERS:
        send(2, o, b_mine, b_mine)

    def project(group):
        weight = qw_v[:, pl.ds(pl.multiple_of(group * GROUP_WIDTH, GROUP_WIDTH), GROUP_WIDTH)]
        return lax.dot_general(normed[group], weight, NT, preferred_element_type=F32)

    fetches["qw"].wait()
    fetches["vup"].wait()
    fetches["kvw"].wait()
    query_own = added([project(k * NC + c) for k in range(NX)])
    c_msg[0, :, pl.ds(0, HALF)] = query_own
    query_parts = [c_msg[0, :, pl.ds(0, HALF)]]
    for k in range(NX):
        group = at_y[k] * NC + 1 - c
        pltpu.make_async_copy(normed.at[group], normed.at[group], half_sem.at[k]).wait()
        query_parts.append(project(group))
    query_plain = added(query_parts)
    seq_width = MODEL_WIDTH // SEQ
    seq_start = pl.multiple_of(lax.rem(z, 4) * seq_width, seq_width)
    keyval_part = jnp.dot(
        normed[x * NC + z // 4, :, pl.ds(seq_start, seq_width)], kvw_v[...], preferred_element_type=F32
    )
    query_lanes = lane // HALF == lax.rem(z, 2)
    plain = jnp.concatenate([query_plain, query_plain], axis=1)
    for k in range(4):
        quarter = keyval_part[:, k * HALF : (k + 1) * HALF]
        c_msg[k] = jnp.where(query_lanes, plain, jnp.concatenate([quarter, quarter], axis=1))

    c_buf[pl.ds(seq, 1)] = c_msg[pl.ds(lax.rem(z, 4), 1)]
    for o in SEQ_PARTNERS:
        send(3, o, c_msg.at[lax.rem(z + o[2], 4)], c_buf.at[seq])

    landed(2, b_buf.at[pl.ds(0, GROUPS - 1)])
    low_sum = added([b_buf[k] for k in range(GROUPS)])
    low_rank = jnp.where(chosen, low_sum, 0.0)
    low_query, low_value = low_rank[:, :128], low_rank[:, 128:].astype(BF16)
    low_query = jnp.concatenate([low_query, pltpu.roll(low_query, HALF, 1)], axis=0)[:, :HALF].astype(BF16)
    landed(9, up_buf.at[pl.ds(0, NZ - 1)])
    ring_heads = NZ // 2
    for h in range(ring_heads):
        even = jnp.dot(low_query, up_buf[2 * h], preferred_element_type=F32)
        odd = jnp.dot(low_query, up_buf[2 * h + 1], preferred_element_type=F32)
        crossed = jnp.where(lane < HALF, odd[:ROWS], even[ROWS:])
        query_delta[x * ring_heads + h] = jnp.where(lane < HALF, even[:ROWS], odd[ROWS:]) + pltpu.roll(crossed, HALF, 1)
    ring_delta = query_delta.at[pl.ds(x * ring_heads, ring_heads)]
    for o in XY_PARTNERS:
        if o[1] == 0:
            send(10, o, ring_delta, ring_delta)
    value_delta = jnp.dot(
        low_value, vup_v[...].reshape(ADAPTERS * RANK, HEAD_SIZE), preferred_element_type=F32
    )

    landed(10, query_delta.at[pl.ds(0, (NX - 1) * ring_heads)])
    landed(3, c_buf.at[pl.ds(0, SEQ - 1)])
    pairs = [(c_buf[2 * h], c_buf[2 * h + 1]) for h in range(HEADS)]
    whole = [jnp.where(lane < HALF, even, odd) + query_delta[h] for h, (even, odd) in enumerate(pairs)]
    whole = [t.astype(BF16).astype(F32) for t in whole]
    turned = [t * cosine + pltpu.roll(t, HALF, 1) * signed_sine for t in whole]
    for h in range(HEADS):
        q_rot[pl.ds(h * ROWS, ROWS)] = turned[h].astype(BF16).astype(F32)
    kv_rows[...] = added([even for even, _ in pairs]) + pltpu.roll(added([odd for _, odd in pairs]), HALF, 1)
    kv_piece = jnp.broadcast_to(kv_rows[pl.ds(seq // QUADS, 1)], (HEADS, 128))

    fetches["k"].wait()
    fetches["v"].wait()
    where = seq * SPAN + lax.broadcasted_iota(jnp.int32, (HEADS, SPAN), 1)
    lane_h = lax.broadcasted_iota(jnp.int32, (HEADS, 128), 1)
    rows = [lax.rem(2 * x + k, ROWS) for k in (4, 5, 2, 3, 6, 7, 0, 1)]
    queries = [q_rot[pl.ds(b, HEADS, stride=ROWS)].astype(BF16) for b in rows]
    own = pl.ds(pl.multiple_of(seq * 8, 8), 8)
    parts = ((range(0, 2), (2,)), (range(2, 6), (1, 3)), (range(6, 8), (0,)))
    scores = {}

    def score(some):
        for i in some:
            scores[i] = lax.dot_general(queries[i], k_v[rows[i]], NT, preferred_element_type=F32)

    score(parts[0][0])
    for n, (some, turns) in enumerate(parts):
        if n + 1 < len(parts):
            score(parts[n + 1][0])
        valid = {i: where < length_s[rows[i]] for i in some}
        masked = {i: jnp.where(valid[i], scores[i] * SCORE_SCALE, MASKED) for i in some}
        block_max = {i: jnp.max(masked[i], axis=1, keepdims=True) for i in some}
        weights = {i: jnp.where(valid[i], jnp.exp(masked[i] - block_max[i]), 0.0) for i in some}
        block_total = {i: jnp.sum(weights[i], axis=1, keepdims=True) for i in some}
        block_acc = {i: jnp.dot(weights[i].astype(BF16), v_v[rows[i]], preferred_element_type=F32) for i in some}
        for i in some:
            facts = jnp.where(lane_h < 32, block_max[i], jnp.where(lane_h < 64, block_total[i], kv_piece))
            for k in range(2):
                heads = block_acc[i][8 * k : 8 * k + 8]
                about = pltpu.roll(facts[8 * k : 8 * k + 8], 4, 0)
                d_msg[rows[i] * QUADS + 2 * k] = jnp.where(sub < 4, heads, about)
                d_msg[rows[i] * QUADS + 2 * k + 1] = jnp.where(sub < 4, about, heads)
        for o in SEQ_PARTNERS:
            if o[0] in turns:
                send(4, o, d_msg.at[at_seq[o[0]][o[2]]], d_buf.at[own])
    d_buf[own] = d_msg[pl.ds(seq, 1)].reshape(8, 128)
    landed(4, d_buf.at[pl.ds(0, (SEQ - 1) * 8)])

    row, quad = seq // QUADS, lax.rem(seq, QUADS)
    acc_row = lax.rem(quad, 2) * 4
    facts_row = 4 - acc_row
    quarter = [d_buf[pl.ds(8 * k + facts_row, ROWS, stride=8 * QUADS)] for k in range(4)]
    key_first = quarter[0] * cosine - quarter[1] * sine
    key_second = quarter[1] * cosine + quarter[0] * sine
    key_new = jnp.concatenate([key_first[:, HALF:], key_second[:, HALF:]], axis=1).astype(BF16)
    value_new = (jnp.concatenate([quarter[2][:, HALF:], quarter[3][:, HALF:]], axis=1) + value_delta).astype(BF16)
    kv_ref[:, pl.ds(0, HEAD_SIZE)] = key_new
    kv_ref[:, pl.ds(HEAD_SIZE, HEAD_SIZE)] = value_new

    kv_rows[...] = key_new.astype(F32)
    own_key = kv_rows[pl.ds(row, 1)]
    kv_rows[...] = value_new.astype(F32)
    own_value = kv_rows[pl.ds(row, 1)]
    own_queries = q_rot[pl.ds(quad * 4 * ROWS + row, 4, stride=ROWS)]
    self_score = jnp.sum(own_queries * own_key, axis=1, keepdims=True) * SCORE_SCALE
    four = range(4)
    acc = [d_buf[pl.ds(acc_row + j, SEQ, stride=8)] for j in four]
    facts = [d_buf[pl.ds(facts_row + j, SEQ, stride=8)] for j in four]
    peaks = [jnp.broadcast_to(facts[j][:, :1], (SEQ, 128)) for j in four]
    own_score = [jnp.broadcast_to(self_score[j : j + 1], (1, 128)) for j in four]
    highest = [jnp.maximum(jnp.max(peaks[j], axis=0, keepdims=True), own_score[j]) for j in four]
    factor = [jnp.exp(peaks[j] - highest[j]) for j in four]
    self_weight = [jnp.exp(own_score[j] - highest[j]) for j in four]
    summed = [jnp.sum(factor[j] * facts[j], axis=0, keepdims=True) for j in four]
    summed = [jnp.broadcast_to(summed[j][:, 32:33], (1, 128)) + self_weight[j] for j in four]
    weighted = [jnp.sum(factor[j] * acc[j], axis=0, keepdims=True) + self_weight[j] * own_value for j in four]
    e_rows = [weighted[j] / summed[j] for j in four]
    attended_own = jnp.concatenate(e_rows + e_rows, axis=0).astype(BF16).astype(F32)
    e_buf[own] = attended_own
    for o in SEQ_PARTNERS:
        send(5, o, e_buf.at[own], e_buf.at[own])
    fetches["ow"].wait()
    landed(5, e_buf.at[pl.ds(0, (SEQ - 1) * 8)])

    attended = jnp.concatenate(
        [e_buf[pl.ds(8 * (h // 4) + h % 4, ROWS, stride=8 * QUADS)] for h in range(HEADS)], axis=1
    ).astype(BF16)
    partial = jnp.dot(attended, ow_v[...], preferred_element_type=F32)
    for k in range(GROUPS):
        tile = partial[:, 128 * (k // 2) : 128 * (k // 2) + 128]
        if k % 2:
            tile = pltpu.roll(tile, HALF, 1)
        f_msg[k] = tile
    f_buf[pl.ds(head, 1)] = f_msg[pl.ds(head, 1)]
    for o in HEAD_PARTNERS:
        send(6, o, f_msg.at[at_head[o[1]][o[3]]], f_buf.at[head])
    landed(6, f_buf.at[pl.ds(0, GROUPS - 1)])
    total = f_buf[0]
    for k in range(1, GROUPS):
        total = total + f_buf[k]
    out_ref[...] = total[:, :HALF].astype(BF16)
    for phase, ref in sent:
        pltpu.make_async_copy(ref, ref, send_sem.at[phase]).wait()


def write_out(delta_ref, keyval_ref, delta_hbm, keyval_hbm, sem):
    first = pltpu.make_async_copy(delta_ref, delta_hbm, sem.at[0])
    second = pltpu.make_async_copy(keyval_ref, keyval_hbm, sem.at[1])
    first.start()
    second.start()
    first.wait()
    second.wait()


def local(
    residual_input,
    norm_gain_vector,
    query_weight,
    key_value_weight,
    output_weight,
    adapter_down_factors,
    query_up_factors,
    value_up_factors,
    adapter_index,
    lengths,
    rotated_key_cache,
    earlier_value_cache,
):
    with jax.ensure_compile_time_eval():
        frequency = jnp.exp(jnp.arange(HALF, dtype=F32) * (-math.log(ROPE_BASE) / HALF))
        frequency = np.asarray(frequency)
    frequency = jnp.asarray(np.concatenate([frequency, frequency])[None, :])
    operands = (
        residual_input,
        norm_gain_vector,
        jnp.transpose(query_weight, (1, 2, 0)).reshape(HALF, MODEL_WIDTH),
        key_value_weight.reshape(MODEL_WIDTH // SEQ, 2 * HEAD_SIZE),
        output_weight.reshape(HEADS * HEAD_SIZE, MODEL_WIDTH // SEQ),
        jnp.transpose(adapter_down_factors, (0, 2, 1)),
        query_up_factors.reshape(ADAPTERS, RANK, HALF),
        value_up_factors.reshape(ADAPTERS, RANK, HEAD_SIZE),
        adapter_index,
        lengths,
        rotated_key_cache.reshape(ROWS, SPAN, HEAD_SIZE),
        earlier_value_cache.reshape(ROWS, SPAN, HEAD_SIZE),
        frequency,
    )
    dma, vmem = pltpu.SemaphoreType.DMA, pltpu.VMEM
    attn_delta, new_keyval = pl.pallas_call(
        kernel,
        out_shape=(vmem((ROWS, HALF), BF16), vmem((ROWS, 2 * HEAD_SIZE), BF16)),
        in_specs=[pl.BlockSpec(memory_space=pl.ANY)] * len(operands),
        out_specs=(pl.BlockSpec(memory_space=vmem), pl.BlockSpec(memory_space=vmem)),
        scratch_shapes=[
            vmem((ROWS, HALF), BF16),
            vmem((HALF,), BF16),
            vmem((HALF, MODEL_WIDTH), BF16),
            vmem((MODEL_WIDTH // SEQ, 2 * HEAD_SIZE), BF16),
            vmem((HEADS * HEAD_SIZE, MODEL_WIDTH // SEQ), BF16),
            vmem((ADAPTERS, 2 * RANK, MODEL_WIDTH // GROUPS), BF16),
            vmem((ADAPTERS, RANK, HALF), BF16),
            vmem((ADAPTERS, RANK, HEAD_SIZE), BF16),
            pltpu.SMEM((ADAPTERS,), jnp.int32),
            pltpu.SMEM((ROWS,), jnp.int32),
            vmem((ROWS, SPAN, HEAD_SIZE), BF16),
            vmem((ROWS, SPAN, HEAD_SIZE), BF16),
            vmem((1, 128), F32),
            vmem((2 * ROWS, 128), BF16),
            vmem((NZ * NC, 2 * ROWS, 128), BF16),
            vmem((NX * NY, NZ // 2 * ROWS, 128), BF16),
            vmem((NX * NY, ROWS, 128), F32),
            vmem((GROUPS, ROWS, GROUP_WIDTH), BF16),
            vmem((GROUPS, ROWS, ADAPTERS * 2 * RANK), F32),
            vmem((4, ROWS, 128), F32),
            vmem((SEQ, ROWS, 128), F32),
            vmem((NZ, ADAPTERS * RANK // 2, 128), BF16),
            vmem((HEADS, ROWS, 128), F32),
            vmem((HEADS * ROWS, 128), F32),
            vmem((SEQ, 8, 128), F32),
            vmem((SEQ * 8, 128), F32),
            vmem((ROWS, 128), F32),
            vmem((SEQ * 8, 128), F32),
            vmem((GROUPS, ROWS, 128), F32),
            vmem((GROUPS, ROWS, 128), F32),
            dma((13,)),
            dma((11,)),
            dma((11,)),
            dma((NX * NY,)),
            dma((NX,)),
        ],
        compiler_params=pltpu.CompilerParams(
            collective_id=0, has_side_effects=True, vmem_limit_bytes=62 * 2**20
        ),
        name="decode_attention",
    )(*operands)
    attn_delta, new_keyval = pl.pallas_call(
        write_out,
        out_shape=(
            jax.ShapeDtypeStruct((ROWS, HALF), BF16),
            jax.ShapeDtypeStruct((ROWS, 2 * HEAD_SIZE), BF16),
        ),
        in_specs=[pl.BlockSpec(memory_space=vmem)] * 2,
        out_specs=[pl.BlockSpec(memory_space=pl.ANY)] * 2,
        scratch_shapes=[dma((2,))],
        compiler_params=pltpu.CompilerParams(vmem_limit_bytes=2**20),
        name="write_out",
    )(attn_delta, new_keyval)
    return attn_delta, new_keyval[:, None, :]


def solution(mesh):
    return jax.shard_map(
        local,
        mesh=mesh,
        in_specs=(
            P(None, ("kvseq", "kvhead")),
            P(("kvseq", "kvhead")),
            P(None, "kvhead", "kvseq"),
            P("kvseq", "kvhead", None),
            P("kvhead", None, "kvseq"),
            P(None, "kvhead", None),
            P(None, None, "kvhead", "kvseq"),
            P(None, None, "kvhead", None),
            P(),
            P(),
            P(None, "kvseq", "kvhead", None),
            P(None, "kvseq", "kvhead", None),
        ),
        out_specs=(P(None, ("kvseq", "kvhead")), P(None, "kvhead", None)),
        check_vma=False,
    )
```

```python
import math

import jax
import jax.numpy as jnp
import numpy as np
from jax import lax
from jax.experimental import pallas as pl
from jax.experimental.pallas import tpu as pltpu
from jax.sharding import PartitionSpec as P

MODEL_WIDTH = 16384
HEADS = 16
HEAD_SIZE = 128
HALF = HEAD_SIZE // 2
ADAPTERS = 8
RANK = 16
ROWS = 8
SPAN = 1024
NX, NY, NZ, NC = 4, 4, 8, 2
SEQ = NX * NZ
GROUPS = NY * NC
QUADS = SEQ // ROWS
GROUP_WIDTH = MODEL_WIDTH // GROUPS

EPSILON = 1e-05
ROPE_BASE = 500000.0
MASKED = -1e30
SCORE_SCALE = 1.0 / math.sqrt(HEAD_SIZE)
MESH = pl.DeviceIdType.MESH
F32 = jnp.float32
BF16 = jnp.bfloat16
NT = (((1,), (1,)), ((), ()))


def ring(k, n):
    return min(k, n - k)


def added(terms):
    while len(terms) > 1:
        terms = [sum(terms[k + 1 : k + 2], terms[k]) for k in range(0, len(terms), 2)]
    return terms[0]


def far_first(o):
    return -(ring(o[0], NX) + ring(o[1], NY) + ring(o[2], NZ)), -o[3]


def offsets(xs, ys, zs, cs):
    found = [(x, y, z, c) for x in xs for y in ys for z in zs for c in cs if (x, y, z, c) != (0, 0, 0, 0)]
    return sorted(found, key=far_first)


Z_PARTNERS = offsets([0], [0], range(NZ), range(NC))
XY_PARTNERS = offsets(range(NX), range(NY), [0], [0])
HEAD_PARTNERS = offsets([0], range(NY), [0], range(NC))
SEQ_PARTNERS = offsets(range(NX), [0], range(NZ), [0])


def kernel(
    x_hbm, gain_hbm, qw_hbm, kvw_hbm, ow_hbm, down_hbm, qup_hbm, vup_hbm, adapter_hbm, length_hbm, k_hbm, v_hbm, freq_hbm,
    out_ref, kv_ref,
    x_v, gain_v, qw_v, kvw_v, ow_v, down_v, qup_v, vup_v, adapter_s, length_s, k_v, v_v, freq_v,
    z_msg, z_buf, xy_buf, sq_buf, normed, b_buf, c_msg, c_buf, up_buf, query_delta, q_rot, d_msg, d_buf, kv_rows, e_buf, f_msg, f_buf,
    local_sem, send_sem, recv_sem, xy_sem, half_sem,
):
    seq, head = lax.axis_index("kvseq"), lax.axis_index("kvhead")
    x, z = seq // NZ, lax.rem(seq, NZ)
    y, c = head // NC, lax.rem(head, NC)

    at_x = [lax.rem(x + k, NX) for k in range(NX)]
    at_y = [lax.rem(y + k, NY) for k in range(NY)]
    at_z = [lax.rem(z + k, NZ) for k in range(NZ)]
    at_c = [c, 1 - c]
    at_seq = [[at_x[i] * NZ + at_z[k] for k in range(NZ)] for i in range(NX)]
    at_head = [[at_y[i] * NC + at_c[k] for k in range(NC)] for i in range(NY)]

    def place(o):
        return at_seq[o[0]][o[2]], at_head[o[1]][o[3]]

    barrier = pltpu.get_barrier_semaphore()
    for o in sorted(XY_PARTNERS + Z_PARTNERS, key=far_first):
        pl.semaphore_signal(barrier, inc=1, device_id=place(o), device_id_type=MESH)

    fetches = {}

    def fetch(name, src, dst):
        fetches[name] = pltpu.make_async_copy(src, dst, local_sem.at[len(fetches)])
        fetches[name].start()

    fetch("x", x_hbm, x_v)
    fetch("gain", gain_hbm, gain_v)
    fetch("length", length_hbm, length_s)
    fetch("adapter", adapter_hbm, adapter_s)
    fetch("freq", freq_hbm, freq_v)
    fetch("qup", qup_hbm, qup_v)

    sent = []

    def send_to(phase, device, src, dst, sem):
        copy = pltpu.make_async_remote_copy(
            src_ref=src, dst_ref=dst, send_sem=send_sem.at[phase], recv_sem=sem, device_id=device, device_id_type=MESH
        )
        copy.start()

    def send(phase, o, src, dst):
        send_to(phase, place(o), src, dst, recv_sem.at[phase])

    def landed(phase, ref):
        pltpu.make_async_copy(ref, ref, recv_sem.at[phase]).wait()
        sent.append((phase, ref))

    lane = lax.broadcasted_iota(jnp.int32, (ROWS, 128), 1)
    sub = lax.broadcasted_iota(jnp.int32, (ROWS, 128), 0)

    fetches["x"].wait()
    fetches["gain"].wait()
    mine = x_v[...].astype(F32)
    gains = jnp.broadcast_to(gain_v[...].astype(F32).reshape(1, HALF), (ROWS, HALF))
    both = jnp.concatenate([mine, jnp.where(sub[:, :HALF] == 0, gains, 0.0)], axis=0)
    both = jnp.concatenate([both, both], axis=1)
    lane2 = lax.broadcasted_iota(jnp.int32, (2 * ROWS, 128), 1)
    block = jnp.where(lane2 // HALF == c, both, 0.0).astype(BF16)
    z_msg[...] = block
    z_buf[pl.ds(z * NC + c, 1)] = block[None]

    pl.semaphore_wait(barrier, len(XY_PARTNERS) + len(Z_PARTNERS))
    for o in Z_PARTNERS:
        send(0, o, z_msg, z_buf.at[z * NC + c])
    fetch("down", down_hbm, down_v)
    fetch("kvw", kvw_hbm, kvw_v)
    fetch("qw", qw_hbm, qw_v)
    fetch("vup", vup_hbm, vup_v)
    fetch("k", k_hbm, k_v)
    fetch("v", v_hbm, v_v)
    fetch("ow", ow_hbm, ow_v)

    fetches["length"].wait()
    fetches["freq"].wait()
    fetches["adapter"].wait()
    position = jnp.zeros((ROWS, 128), F32)
    adapter = jnp.zeros((ROWS, ADAPTERS * 2 * RANK), jnp.int32)
    sub_wide = lax.broadcasted_iota(jnp.int32, adapter.shape, 0)
    for b in range(ROWS):
        position = jnp.where(sub == b, length_s[b].astype(F32), position)
        adapter = jnp.where(sub_wide == b, adapter_s[b], adapter)
    chosen = adapter == lax.rem(lax.broadcasted_iota(jnp.int32, adapter.shape, 1), ADAPTERS * RANK) // RANK
    angles = position * freq_v[...]
    cosine, sine = jnp.cos(angles), jnp.sin(angles)
    signed_sine = jnp.where(lane < HALF, -sine, sine)

    landed(0, z_buf.at[pl.ds(0, NZ * NC - 1)])
    tiles = [z_buf[2 * k].astype(F32) + z_buf[2 * k + 1].astype(F32) for k in range(NZ)]
    squares = added([tile[:ROWS] * tile[:ROWS] for tile in tiles])
    facts = squares + pltpu.roll(squares, HALF, 1)
    half = [jnp.where(c == 0, tiles[k], tiles[k + NZ // 2]) for k in range(NZ // 2)]
    for k in range(NZ // 2):
        gain_k = half[k][ROWS : ROWS + 1]
        facts = jnp.where((sub == 2 * k) & (lane >= HALF), pltpu.roll(gain_k, HALF, 1), facts)
        facts = jnp.where((sub == 2 * k + 1) & (lane >= HALF), gain_k, facts)
    here = x * NY + y
    xy_mine = xy_buf.at[here]
    sq_mine = sq_buf.at[here]
    sq_mine[...] = facts
    for o in XY_PARTNERS:
        send(1, o, sq_mine, sq_mine)
    xy_mine[...] = jnp.concatenate([t[:ROWS] for t in half], axis=0).astype(BF16)
    for o in XY_PARTNERS:
        send_to(7, place(o), xy_mine, xy_mine, xy_sem.at[here])
    sent.append((7, xy_buf.at[pl.ds(0, NX * NY - 1)]))

    fetches["qup"].wait()
    query_up = qup_v[...].reshape(ADAPTERS * RANK, HALF)
    up_buf[z] = jnp.concatenate([query_up[: ADAPTERS * RANK // 2], query_up[ADAPTERS * RANK // 2 :]], axis=1)
    for o in Z_PARTNERS:
        if o[3] == 0:
            send(9, o, up_buf.at[z], up_buf.at[z])

    def arrived(k):
        pltpu.make_async_copy(xy_buf.at[k], xy_buf.at[k], xy_sem.at[k]).wait()

    landed(1, sq_buf.at[pl.ds(0, NX * NY - 1)])
    square_sum = added([sq_buf[k] for k in range(NX * NY)])
    square_sum = jnp.sum(jnp.where(lane < HALF, square_sum, 0.0), axis=1, keepdims=True)
    scaling = jnp.broadcast_to(lax.rsqrt(square_sum / MODEL_WIDTH + EPSILON), (ROWS, 128))
    scaling = jnp.concatenate([scaling, scaling], axis=0)

    def normalize(kx):
        for ky in range(NY):
            pl.when(kx * NY + ky != here)(lambda ky=ky: arrived(kx * NY + ky))
        group = kx * NC + c
        for ky in range(NY):
            k = kx * NY + ky
            gain_odd = sq_buf[k]
            gain_even = pltpu.roll(gain_odd, HALF, 1)
            for p in range(2):
                part = xy_buf[k, pl.ds(p * 2 * ROWS, 2 * ROWS)].astype(F32) * scaling
                for i in range(2):
                    n = 2 * p + i
                    gain_row = jnp.where(lane[:1] < HALF, gain_even[2 * n : 2 * n + 1], gain_odd[2 * n + 1 : 2 * n + 2])
                    one = part[i * ROWS : (i + 1) * ROWS] * gain_row
                    normed[group, :, pl.ds((n * NY + ky) * 128, 128)] = one.astype(BF16)

    other = (0, 0, 0, 1)
    by_distance = [at_x[k] for k in (0, 1, 3, 2)]
    for k in range(NX):
        normalize(by_distance[k])
        group = by_distance[k] * NC + c
        send_to(8, place(other), normed.at[group], normed.at[group], half_sem.at[k])
    sent.append((8, normed.at[pl.ds(0, NX)]))

    fetches["down"].wait()
    b_mine = b_buf.at[head]
    for k in range(2):
        factors = down_v[:, k * RANK : (k + 1) * RANK].reshape(ADAPTERS * RANK, GROUP_WIDTH)
        b_mine[:, pl.ds(k * 128, 128)] = lax.dot_general(normed[head], factors, NT, preferred_element_type=F32)
    for o in HEAD_PARTNERS:
        send(2, o, b_mine, b_mine)

    def project(group):
        weight = qw_v[:, pl.ds(pl.multiple_of(group * GROUP_WIDTH, GROUP_WIDTH), GROUP_WIDTH)]
        return lax.dot_general(normed[group], weight, NT, preferred_element_type=F32)

    fetches["qw"].wait()
    fetches["vup"].wait()
    fetches["kvw"].wait()
    query_own = added([project(k * NC + c) for k in range(NX)])
    c_msg[0, :, pl.ds(0, HALF)] = query_own
    query_parts = [c_msg[0, :, pl.ds(0, HALF)]]
    for k in range(NX):
        group = by_distance[k] * NC + 1 - c
        pltpu.make_async_copy(normed.at[group], normed.at[group], half_sem.at[k]).wait()
        query_parts.append(project(group))
    query_plain = added(query_parts)
    seq_width = MODEL_WIDTH // SEQ
    seq_start = pl.multiple_of(lax.rem(z, 4) * seq_width, seq_width)
    keyval_part = jnp.dot(
        normed[x * NC + z // 4, :, pl.ds(seq_start, seq_width)], kvw_v[...], preferred_element_type=F32
    )
    query_lanes = lane // HALF == lax.rem(z, 2)
    plain = jnp.concatenate([query_plain, query_plain], axis=1)
    for k in range(4):
        quarter = keyval_part[:, k * HALF : (k + 1) * HALF]
        c_msg[k] = jnp.where(query_lanes, plain, jnp.concatenate([quarter, quarter], axis=1))

    c_buf[pl.ds(seq, 1)] = c_msg[pl.ds(lax.rem(z, 4), 1)]
    for o in SEQ_PARTNERS:
        send(3, o, c_msg.at[lax.rem(z + o[2], 4)], c_buf.at[seq])

    landed(2, b_buf.at[pl.ds(0, GROUPS - 1)])
    low_sum = added([b_buf[k] for k in range(GROUPS)])
    low_rank = jnp.where(chosen, low_sum, 0.0)
    low_query, low_value = low_rank[:, :128], low_rank[:, 128:].astype(BF16)
    low_query = jnp.concatenate([low_query, pltpu.roll(low_query, HALF, 1)], axis=0)[:, :HALF].astype(BF16)
    landed(9, up_buf.at[pl.ds(0, NZ - 1)])
    ring_heads = NZ // 2
    for h in range(ring_heads):
        even = jnp.dot(low_query, up_buf[2 * h], preferred_element_type=F32)
        odd = jnp.dot(low_query, up_buf[2 * h + 1], preferred_element_type=F32)
        crossed = jnp.where(lane < HALF, odd[:ROWS], even[ROWS:])
        query_delta[x * ring_heads + h] = jnp.where(lane < HALF, even[:ROWS], odd[ROWS:]) + pltpu.roll(crossed, HALF, 1)
    ring_delta = query_delta.at[pl.ds(x * ring_heads, ring_heads)]
    for o in XY_PARTNERS:
        if o[1] == 0:
            send(10, o, ring_delta, ring_delta)
    value_delta = jnp.dot(
        low_value, vup_v[...].reshape(ADAPTERS * RANK, HEAD_SIZE), preferred_element_type=F32
    )

    landed(10, query_delta.at[pl.ds(0, (NX - 1) * ring_heads)])
    landed(3, c_buf.at[pl.ds(0, SEQ - 1)])
    pairs = [(c_buf[2 * h], c_buf[2 * h + 1]) for h in range(HEADS)]
    whole = [jnp.where(lane < HALF, even, odd) + query_delta[h] for h, (even, odd) in enumerate(pairs)]
    whole = [t.astype(BF16).astype(F32) for t in whole]
    turned = [t * cosine + pltpu.roll(t, HALF, 1) * signed_sine for t in whole]
    for h in range(HEADS):
        q_rot[pl.ds(h * ROWS, ROWS)] = turned[h].astype(BF16).astype(F32)
    kv_rows[...] = added([even for even, _ in pairs]) + pltpu.roll(added([odd for _, odd in pairs]), HALF, 1)
    kv_piece = jnp.broadcast_to(kv_rows[pl.ds(seq // QUADS, 1)], (HEADS, 128))

    fetches["k"].wait()
    fetches["v"].wait()
    where = seq * SPAN + lax.broadcasted_iota(jnp.int32, (HEADS, SPAN), 1)
    lane_h = lax.broadcasted_iota(jnp.int32, (HEADS, 128), 1)
    rows = [lax.rem(2 * x + k, ROWS) for k in (4, 5, 2, 3, 6, 7, 0, 1)]
    queries = [q_rot[pl.ds(b, HEADS, stride=ROWS)].astype(BF16) for b in rows]
    own = pl.ds(pl.multiple_of(seq * 8, 8), 8)
    parts = ((range(0, 2), (2,)), (range(2, 6), (1, 3)), (range(6, 8), (0,)))
    scores = {}

    def score(some):
        for i in some:
            scores[i] = lax.dot_general(queries[i], k_v[rows[i]], NT, preferred_element_type=F32)

    score(parts[0][0])
    for n, (some, turns) in enumerate(parts):
        if n + 1 < len(parts):
            score(parts[n + 1][0])
        valid = {i: where < length_s[rows[i]] for i in some}
        masked = {i: jnp.where(valid[i], scores[i] * SCORE_SCALE, MASKED) for i in some}
        block_max = {i: jnp.max(masked[i], axis=1, keepdims=True) for i in some}
        weights = {i: jnp.where(valid[i], jnp.exp(masked[i] - block_max[i]), 0.0) for i in some}
        block_total = {i: jnp.sum(weights[i], axis=1, keepdims=True) for i in some}
        block_acc = {i: jnp.dot(weights[i].astype(BF16), v_v[rows[i]], preferred_element_type=F32) for i in some}
        for i in some:
            facts = jnp.where(lane_h < 32, block_max[i], jnp.where(lane_h < 64, block_total[i], kv_piece))
            for k in range(2):
                heads = block_acc[i][8 * k : 8 * k + 8]
                about = pltpu.roll(facts[8 * k : 8 * k + 8], 4, 0)
                d_msg[rows[i] * QUADS + 2 * k] = jnp.where(sub < 4, heads, about)
                d_msg[rows[i] * QUADS + 2 * k + 1] = jnp.where(sub < 4, about, heads)
        for o in SEQ_PARTNERS:
            if o[0] in turns:
                send(4, o, d_msg.at[at_seq[o[0]][o[2]]], d_buf.at[own])
    d_buf[own] = d_msg[pl.ds(seq, 1)].reshape(8, 128)
    landed(4, d_buf.at[pl.ds(0, (SEQ - 1) * 8)])

    row, quad = seq // QUADS, lax.rem(seq, QUADS)
    acc_row = lax.rem(quad, 2) * 4
    facts_row = 4 - acc_row
    quarter = [d_buf[pl.ds(8 * k + facts_row, ROWS, stride=8 * QUADS)] for k in range(4)]
    key_first = quarter[0] * cosine - quarter[1] * sine
    key_second = quarter[1] * cosine + quarter[0] * sine
    key_new = jnp.concatenate([key_first[:, HALF:], key_second[:, HALF:]], axis=1).astype(BF16)
    value_new = (jnp.concatenate([quarter[2][:, HALF:], quarter[3][:, HALF:]], axis=1) + value_delta).astype(BF16)
    kv_ref[:, pl.ds(0, HEAD_SIZE)] = key_new
    kv_ref[:, pl.ds(HEAD_SIZE, HEAD_SIZE)] = value_new

    kv_rows[...] = key_new.astype(F32)
    own_key = kv_rows[pl.ds(row, 1)]
    kv_rows[...] = value_new.astype(F32)
    own_value = kv_rows[pl.ds(row, 1)]
    own_queries = q_rot[pl.ds(quad * 4 * ROWS + row, 4, stride=ROWS)]
    self_score = jnp.sum(own_queries * own_key, axis=1, keepdims=True) * SCORE_SCALE
    four = range(4)
    acc = [d_buf[pl.ds(acc_row + j, SEQ, stride=8)] for j in four]
    facts = [d_buf[pl.ds(facts_row + j, SEQ, stride=8)] for j in four]
    peaks = [jnp.broadcast_to(facts[j][:, :1], (SEQ, 128)) for j in four]
    own_score = [jnp.broadcast_to(self_score[j : j + 1], (1, 128)) for j in four]
    highest = [jnp.maximum(jnp.max(peaks[j], axis=0, keepdims=True), own_score[j]) for j in four]
    factor = [jnp.exp(peaks[j] - highest[j]) for j in four]
    self_weight = [jnp.exp(own_score[j] - highest[j]) for j in four]
    summed = [jnp.sum(factor[j] * facts[j], axis=0, keepdims=True) for j in four]
    summed = [jnp.broadcast_to(summed[j][:, 32:33], (1, 128)) + self_weight[j] for j in four]
    weighted = [jnp.sum(factor[j] * acc[j], axis=0, keepdims=True) + self_weight[j] * own_value for j in four]
    e_rows = [weighted[j] / summed[j] for j in four]
    attended_own = jnp.concatenate(e_rows + e_rows, axis=0).astype(BF16).astype(F32)
    e_buf[own] = attended_own
    for o in SEQ_PARTNERS:
        send(5, o, e_buf.at[own], e_buf.at[own])
    fetches["ow"].wait()
    landed(5, e_buf.at[pl.ds(0, (SEQ - 1) * 8)])

    attended = jnp.concatenate(
        [e_buf[pl.ds(8 * (h // 4) + h % 4, ROWS, stride=8 * QUADS)] for h in range(HEADS)], axis=1
    ).astype(BF16)
    width = MODEL_WIDTH // SEQ // 2
    for far in (True, False):
        pair = 1 - y // 2 if far else y // 2
        columns = pl.ds(pl.multiple_of(pair * width, width), width)
        partial = jnp.dot(attended, ow_v[:, columns], preferred_element_type=F32)
        for k in range(GROUPS // 2):
            tile = partial[:, 128 * (k // 2) : 128 * (k // 2) + 128]
            if k % 2:
                tile = pltpu.roll(tile, HALF, 1)
            f_msg[pair * (GROUPS // 2) + k] = tile
        same, crossed = pair * 2 + lax.rem(y, 2), pair * 2 + 1 - lax.rem(y, 2)
        targets = [(same, 1), (same, 0), (crossed, 1), (crossed, 0)] if far else [(crossed, 1), (crossed, 0), (same, 1)]
        for to_y, to_c in targets:
            to = to_y * NC + at_c[to_c]
            send_to(6, (seq, to), f_msg.at[to], f_buf.at[head], recv_sem.at[6])
    f_buf[pl.ds(head, 1)] = f_msg[pl.ds(head, 1)]
    landed(6, f_buf.at[pl.ds(0, GROUPS - 1)])
    total = f_buf[0]
    for k in range(1, GROUPS):
        total = total + f_buf[k]
    out_ref[...] = total[:, :HALF].astype(BF16)
    for phase, ref in sent:
        pltpu.make_async_copy(ref, ref, send_sem.at[phase]).wait()


def write_out(delta_ref, keyval_ref, delta_hbm, keyval_hbm, sem):
    first = pltpu.make_async_copy(delta_ref, delta_hbm, sem.at[0])
    second = pltpu.make_async_copy(keyval_ref, keyval_hbm, sem.at[1])
    first.start()
    second.start()
    first.wait()
    second.wait()


def local(
    residual_input,
    norm_gain_vector,
    query_weight,
    key_value_weight,
    output_weight,
    adapter_down_factors,
    query_up_factors,
    value_up_factors,
    adapter_index,
    lengths,
    rotated_key_cache,
    earlier_value_cache,
):
    with jax.ensure_compile_time_eval():
        frequency = jnp.exp(jnp.arange(HALF, dtype=F32) * (-math.log(ROPE_BASE) / HALF))
        frequency = np.asarray(frequency)
    frequency = jnp.asarray(np.concatenate([frequency, frequency])[None, :])
    operands = (
        residual_input,
        norm_gain_vector,
        jnp.transpose(query_weight, (1, 2, 0)).reshape(HALF, MODEL_WIDTH),
        key_value_weight.reshape(MODEL_WIDTH // SEQ, 2 * HEAD_SIZE),
        output_weight.reshape(HEADS * HEAD_SIZE, MODEL_WIDTH // SEQ),
        jnp.transpose(adapter_down_factors, (0, 2, 1)),
        query_up_factors.reshape(ADAPTERS, RANK, HALF),
        value_up_factors.reshape(ADAPTERS, RANK, HEAD_SIZE),
        adapter_index,
        lengths,
        rotated_key_cache.reshape(ROWS, SPAN, HEAD_SIZE),
        earlier_value_cache.reshape(ROWS, SPAN, HEAD_SIZE),
        frequency,
    )
    dma, vmem = pltpu.SemaphoreType.DMA, pltpu.VMEM
    attn_delta, new_keyval = pl.pallas_call(
        kernel,
        out_shape=(vmem((ROWS, HALF), BF16), vmem((ROWS, 2 * HEAD_SIZE), BF16)),
        in_specs=[pl.BlockSpec(memory_space=pl.ANY)] * len(operands),
        out_specs=(pl.BlockSpec(memory_space=vmem), pl.BlockSpec(memory_space=vmem)),
        scratch_shapes=[
            vmem((ROWS, HALF), BF16),
            vmem((HALF,), BF16),
            vmem((HALF, MODEL_WIDTH), BF16),
            vmem((MODEL_WIDTH // SEQ, 2 * HEAD_SIZE), BF16),
            vmem((HEADS * HEAD_SIZE, MODEL_WIDTH // SEQ), BF16),
            vmem((ADAPTERS, 2 * RANK, MODEL_WIDTH // GROUPS), BF16),
            vmem((ADAPTERS, RANK, HALF), BF16),
            vmem((ADAPTERS, RANK, HEAD_SIZE), BF16),
            pltpu.SMEM((ADAPTERS,), jnp.int32),
            pltpu.SMEM((ROWS,), jnp.int32),
            vmem((ROWS, SPAN, HEAD_SIZE), BF16),
            vmem((ROWS, SPAN, HEAD_SIZE), BF16),
            vmem((1, 128), F32),
            vmem((2 * ROWS, 128), BF16),
            vmem((NZ * NC, 2 * ROWS, 128), BF16),
            vmem((NX * NY, NZ // 2 * ROWS, 128), BF16),
            vmem((NX * NY, ROWS, 128), F32),
            vmem((GROUPS, ROWS, GROUP_WIDTH), BF16),
            vmem((GROUPS, ROWS, ADAPTERS * 2 * RANK), F32),
            vmem((4, ROWS, 128), F32),
            vmem((SEQ, ROWS, 128), F32),
            vmem((NZ, ADAPTERS * RANK // 2, 128), BF16),
            vmem((HEADS, ROWS, 128), F32),
            vmem((HEADS * ROWS + 8, 128), F32),
            vmem((SEQ, 8, 128), F32),
            vmem((SEQ * 8 + 32, 128), F32),
            vmem((ROWS, 128), F32),
            vmem((SEQ * 8 + 32, 128), F32),
            vmem((GROUPS, ROWS, 128), F32),
            vmem((GROUPS, ROWS, 128), F32),
            dma((13,)),
            dma((11,)),
            dma((11,)),
            dma((NX * NY,)),
            dma((NX,)),
        ],
        compiler_params=pltpu.CompilerParams(
            collective_id=0, has_side_effects=True, vmem_limit_bytes=62 * 2**20
        ),
        name="decode_attention",
    )(*operands)
    attn_delta, new_keyval = pl.pallas_call(
        write_out,
        out_shape=(
            jax.ShapeDtypeStruct((ROWS, HALF), BF16),
            jax.ShapeDtypeStruct((ROWS, 2 * HEAD_SIZE), BF16),
        ),
        in_specs=[pl.BlockSpec(memory_space=vmem)] * 2,
        out_specs=[pl.BlockSpec(memory_space=pl.ANY)] * 2,
        scratch_shapes=[dma((2,))],
        compiler_params=pltpu.CompilerParams(vmem_limit_bytes=2**20),
        name="write_out",
    )(attn_delta, new_keyval)
    return attn_delta, new_keyval[:, None, :]


def solution(mesh):
    return jax.shard_map(
        local,
        mesh=mesh,
        in_specs=(
            P(None, ("kvseq", "kvhead")),
            P(("kvseq", "kvhead")),
            P(None, "kvhead", "kvseq"),
            P("kvseq", "kvhead", None),
            P("kvhead", None, "kvseq"),
            P(None, "kvhead", None),
            P(None, None, "kvhead", "kvseq"),
            P(None, None, "kvhead", None),
            P(),
            P(),
            P(None, "kvseq", "kvhead", None),
            P(None, "kvseq", "kvhead", None),
        ),
        out_specs=(P(None, ("kvseq", "kvhead")), P(None, "kvhead", None)),
        check_vma=False,
    )
```
